32 devices in a mesh: rep: 2 (over x), shard: 16 (over z, y, core).
Axes of the slice: x: 2, y: 2, z: 4, core: 2. Of those that a mesh axis runs over, the one named last changes fastest.
Arguments:
- tokens: bfloat16 [64, 256, 768], P(('rep', 'shard')), may hold values from -6 to 6
- condition: float32 [64, 768], P(('rep', 'shard')), may hold values from -6 to 6
- cotangent: bfloat16 [64, 256, 768], P(('rep', 'shard')), may hold values from -6 to 6
- w_ada: float32 [2, 768, 4608], P(None, 'shard'), may hold values from -0.21875 to 0.21875
- b_ada: float32 [2, 6, 768], P(None, None, 'shard'), may hold values from -1.2 to 3.2
- w_qkv: float32 [2, 768, 2304], P(None, 'shard'), may hold values from -0.15625 to 0.15625
- w_proj: float32 [2, 768, 768], P(None, 'shard'), may hold values from -0.875 to 0.875
- w_fc1: float32 [2, 768, 3072], P(None, 'shard'), may hold values from -0.15625 to 0.15625
- w_fc2: float32 [2, 3072, 768], P(None, 'shard'), may hold values from -0.109375 to 0.109375
- first_ada: float32 [2, 768, 4608], P(None, 'shard'), may hold values from -0.875 to 0.875
- first_bias: float32 [2, 6, 768], P(None, None, 'shard'), may hold values from -0.875 to 0.875
- first_qkv: float32 [2, 768, 2304], P(None, 'shard'), may hold values from -0.875 to 0.875
- first_proj: float32 [2, 768, 768], P(None, 'shard'), may hold values from -0.875 to 0.875
- first_fc1: float32 [2, 768, 3072], P(None, 'shard'), may hold values from -0.875 to 0.875
- first_fc2: float32 [2, 3072, 768], P(None, 'shard'), may hold values from -0.875 to 0.875
- second_ada: float32 [2, 768, 4608], P(None, 'shard'), may hold values from 0.013 to 0.053
- second_bias: float32 [2, 6, 768], P(None, None, 'shard'), may hold values from 0.013 to 0.053
- second_qkv: float32 [2, 768, 2304], P(None, 'shard'), may hold values from 0.013 to 0.053
- second_proj: float32 [2, 768, 768], P(None, 'shard'), may hold values from 0.013 to 0.053
- second_fc1: float32 [2, 768, 3072], P(None, 'shard'), may hold values from 0.013 to 0.053
- second_fc2: float32 [2, 3072, 768], P(None, 'shard'), may hold values from 0.013 to 0.053
Outputs:
- output_tokens: bfloat16 [64, 256, 768], P(('rep', 'shard'))
- grad_tokens: float32 [64, 256, 768], P(('rep', 'shard'))
- grad_condition: float32 [64, 768], P(('rep', 'shard'))
- new_ada: float32 [2, 768, 4608], P(None, 'shard')
- new_bias: float32 [2, 6, 768], P(None, None, 'shard')
- new_qkv: float32 [2, 768, 2304], P(None, 'shard')
- new_proj: float32 [2, 768, 768], P(None, 'shard')
- new_fc1: float32 [2, 768, 3072], P(None, 'shard')
- new_fc2: float32 [2, 3072, 768], P(None, 'shard')
- next_first_ada: float32 [2, 768, 4608], P(None, 'shard')
- next_first_bias: float32 [2, 6, 768], P(None, None, 'shard')
- next_first_qkv: float32 [2, 768, 2304], P(None, 'shard')
- next_first_proj: float32 [2, 768, 768], P(None, 'shard')
- next_first_fc1: float32 [2, 768, 3072], P(None, 'shard')
- next_first_fc2: float32 [2, 3072, 768], P(None, 'shard')
- next_second_ada: float32 [2, 768, 4608], P(None, 'shard')
- next_second_bias: float32 [2, 6, 768], P(None, None, 'shard')
- next_second_qkv: float32 [2, 768, 2304], P(None, 'shard')
- next_second_proj: float32 [2, 768, 768], P(None, 'shard')
- next_second_fc1: float32 [2, 768, 3072], P(None, 'shard')
- next_second_fc2: float32 [2, 3072, 768], P(None, 'shard')
- grad_norm: float32 [], replicated
The draws below stay inside these ranges and needn't reach their ends.
All inputs are finite; a program needn't handle non-finite values.
Results may differ from the reference program's by a relative error of at most 0.03.
Values may be sent and summed in bfloat16 or wider, within the bound.
No kernel may reach another device: no remote copies, remote signals or barrier semaphores. Data moves between devices by JAX's collectives and lax.ppermute only.
A program may use at most 256 MiB of HBM per device.

```python
import math
import jax
import jax.numpy as jnp
from jax import lax

D = 768
HEAD_DIM = 64
FF = 3072
SEQ = 256
LAYERS = 2
MICRO = 2
LAT_MB = 1
STEP = 10
LATENTS = 64
PARAMS = 21242880


def draw_condition(key, part):
    key = jax.random.fold_in(key, 11)
    ramp = jnp.arange(D, dtype=jnp.float32) / (D - 1)
    base = jnp.clip(jax.random.normal(key, (LATENTS, D), jnp.float32), -4.0, 4.0)
    return base * (0.5 + ramp)


def draw_b_ada(key, part):
    key = jax.random.fold_in(key, 12)
    ramp = jnp.arange(D, dtype=jnp.float32) / (D - 1)
    base = jnp.clip(0.3 * jax.random.normal(key, (LAYERS, 6, D), jnp.float32), -1.2, 1.2)
    lift = 2.0 * ramp
    nothing = jnp.zeros((D,), jnp.float32)
    whole = jnp.ones((D,), jnp.float32)
    offset = jnp.stack([nothing, lift, whole, nothing, lift, whole])
    return base + offset[None]


def block_scale(key, extent, cuts, least, top_value):
    loudness = 1.0
    for position, parts in cuts:
        draws = jax.random.uniform(jax.random.fold_in(jax.random.fold_in(key, 6), position), (parts,), jnp.float32, least / len(cuts), top_value / len(cuts))
        loudness = loudness * jnp.repeat(jnp.exp(draws), extent[position] // parts).reshape((-1,) + (1,) * (len(extent) - 1 - position))
    return loudness


def noise(rng, dims, scale, bound, shards=(), held_as=jnp.bfloat16):
    drawn = jax.random.normal(rng, dims, jnp.float32) * scale
    if len(shards) > 0:
        drawn = block_scale(rng, dims, shards, -0.22, 0.18) * drawn
    return jnp.clip(drawn, min=-bound, max=bound).astype(held_as)


def setup_inputs(seed: int = 0) -> dict:
    key_list = jax.random.split(jax.random.key(seed), 22)
    return {
        "tokens": noise(key_list[0], (LATENTS, SEQ, D), 1.0, 6.0, ((0, 32),)),
        "condition": draw_condition(jax.random.fold_in(key_list[21], 71), 0),
        "cotangent": noise(key_list[2], (LATENTS, SEQ, D), 1.0, 6.0, ((0, 32),)),
        "w_ada": noise(key_list[3], (LAYERS, D, 6 * D), D ** -0.5, 0.21875, ((1, 16),), jnp.float32),
        "b_ada": draw_b_ada(jax.random.fold_in(key_list[21], 71), 0),
        "w_qkv": noise(key_list[5], (LAYERS, D, 3 * D), (2 * D) ** -0.5, 0.15625, ((1, 16),), jnp.float32),
        "w_proj": noise(key_list[6], (LAYERS, D, D), (D // 16) ** -0.5, 0.875, ((1, 16),), jnp.float32),
        "w_fc1": noise(key_list[7], (LAYERS, D, FF), (2 * D) ** -0.5, 0.15625, ((1, 16),), jnp.float32),
        "w_fc2": noise(key_list[8], (LAYERS, FF, D), FF ** -0.5, 0.109375, ((1, 16),), jnp.float32),
        "first_ada": noise(key_list[9], (LAYERS, D, 6 * D), 0.055, 0.875, ((1, 16),), jnp.float32),
        "first_bias": noise(key_list[10], (LAYERS, 6, D), 0.055, 0.875, ((2, 16),), jnp.float32),
        "first_qkv": noise(key_list[11], (LAYERS, D, 3 * D), 0.055, 0.875, ((1, 16),), jnp.float32),
        "first_proj": noise(key_list[12], (LAYERS, D, D), 0.055, 0.875, ((1, 16),), jnp.float32),
        "first_fc1": noise(key_list[13], (LAYERS, D, FF), 0.055, 0.875, ((1, 16),), jnp.float32),
        "first_fc2": noise(key_list[14], (LAYERS, FF, D), 0.055, 0.875, ((1, 16),), jnp.float32),
        "second_ada": jnp.clip(jnp.exp(math.log(0.053) - 1.40534252 * jax.random.uniform(key_list[15], (LAYERS, D, 6 * D), jnp.float32) ** block_scale(key_list[15], (LAYERS, D, 6 * D), ((1, 16),), -0.2, 0.2)), 0.013, 0.053),
        "second_bias": jnp.clip(jnp.exp(math.log(0.053) - 1.40534252 * jax.random.uniform(key_list[16], (LAYERS, 6, D), jnp.float32) ** block_scale(key_list[16], (LAYERS, 6, D), ((2, 16),), -0.2, 0.2)), 0.013, 0.053),
        "second_qkv": jnp.clip(jnp.exp(math.log(0.053) - 1.40534252 * jax.random.uniform(key_list[17], (LAYERS, D, 3 * D), jnp.float32) ** block_scale(key_list[17], (LAYERS, D, 3 * D), ((1, 16),), -0.2, 0.2)), 0.013, 0.053),
        "second_proj": jnp.clip(jnp.exp(math.log(0.053) - 1.40534252 * jax.random.uniform(key_list[18], (LAYERS, D, D), jnp.float32) ** block_scale(key_list[18], (LAYERS, D, D), ((1, 16),), -0.2, 0.2)), 0.013, 0.053),
        "second_fc1": jnp.clip(jnp.exp(math.log(0.053) - 1.40534252 * jax.random.uniform(key_list[19], (LAYERS, D, FF), jnp.float32) ** block_scale(key_list[19], (LAYERS, D, FF), ((1, 16),), -0.2, 0.2)), 0.013, 0.053),
        "second_fc2": jnp.clip(jnp.exp(math.log(0.053) - 1.40534252 * jax.random.uniform(key_list[20], (LAYERS, FF, D), jnp.float32) ** block_scale(key_list[20], (LAYERS, FF, D), ((1, 16),), -0.2, 0.2)), 0.013, 0.053),
    }


norm_epsilon = 1e-06
first_decay = 0.9
second_decay = 0.95
learn_rates = (0.03, 1.0, 0.03, 0.1, 0.03, 0.03)
weight_decay = 0.1
adam_epsilon = 1e-08
clip_scale = 0.5

@jax.custom_vjp
def low(v):
    return lax.optimization_barrier(v.astype(jnp.bfloat16)).astype(jnp.float32)

@jax.custom_vjp
def low_back(v):
    return v

def low_keep(v):
    return (low(v), None)

def low_pass(kept, grad):
    return (grad,)

def back_keep(v):
    return (v, None)

def back_low(kept, grad):
    return (low(grad),)
low.defvjp(low_keep, low_pass)
low_back.defvjp(back_keep, back_low)

def modulate(stream, shift, scale):
    center = lax.optimization_barrier(jnp.mean(stream, -1, keepdims=True))
    centred = stream - center
    spread = lax.optimization_barrier(jnp.mean(centred * centred, -1, keepdims=True))
    return centred * lax.rsqrt(spread + norm_epsilon) * (1.0 + scale) + shift

def matmul_high(left, right):
    return jnp.matmul(left, right, precision=lax.Precision.HIGHEST)

def ref_block(stream, condition, params):
    w_ada, b_ada, w_qkv, w_proj, w_fc1, w_fc2 = [low(param) for param in params]
    batch, length, width = stream.shape
    heads = width // HEAD_DIM
    cond_act = low(jax.nn.silu(condition))
    modul = (matmul_high(cond_act, w_ada) + b_ada.reshape(-1)).reshape(batch, 6, width)
    pieces = [modul[:, index, None, :] for index in range(6)]
    normed = low(modulate(stream, pieces[0], pieces[1]))
    qkv = low(low_back(matmul_high(normed, w_qkv))).reshape(batch, length, 3, heads, HEAD_DIM)
    query = qkv[:, :, 0]
    keys = qkv[:, :, 1]
    values = qkv[:, :, 2]
    scores = low_back(jnp.einsum('bqhe,bkhe->bhqk', query, keys, precision=lax.Precision.HIGHEST) * HEAD_DIM ** (-0.5))
    probs = low(jax.nn.softmax(scores, axis=-1))
    attended = jnp.einsum('bhqk,bkhe->bqhe', probs, values, precision=lax.Precision.HIGHEST)
    attended = low(low_back(attended.reshape(batch, length, width)))
    branch = low_back(matmul_high(attended, w_proj))
    middle = stream + pieces[2] * branch
    normed_two = low(modulate(middle, pieces[3], pieces[4]))
    upper = low_back(matmul_high(normed_two, w_fc1))
    active = low(jax.nn.gelu(upper, approximate=True))
    mlp_out = low_back(matmul_high(active, w_fc2))
    return middle + pieces[5] * mlp_out

def adam_step(weight, first, second, grad, factor, decay, rate):
    grad = grad * factor
    first_new = first_decay * first + (1.0 - first_decay) * grad
    second_new = second_decay * second + (1.0 - second_decay) * grad * grad
    ratio = first_new / (1.0 - first_decay ** STEP) / (jnp.sqrt(second_new / (1.0 - second_decay ** STEP)) + adam_epsilon)
    return (weight - rate * (ratio + decay * weight), first_new, second_new)

def reference(tokens, condition, cotangent, w_ada, b_ada, w_qkv, w_proj, w_fc1, w_fc2, first_ada, first_bias, first_qkv, first_proj, first_fc1, first_fc2, second_ada, second_bias, second_qkv, second_proj, second_fc1, second_fc2):
    params = (w_ada, b_ada, w_qkv, w_proj, w_fc1, w_fc2)
    firsts = (first_ada, first_bias, first_qkv, first_proj, first_fc1, first_fc2)
    seconds = (second_ada, second_bias, second_qkv, second_proj, second_fc1, second_fc2)
    group = LAT_MB * MICRO
    count = LATENTS // group
    streams = tokens.astype(jnp.float32).reshape(count, group, SEQ, D)
    conds = condition.astype(jnp.float32).reshape(count, group, D)
    backs = cotangent.astype(jnp.float32).reshape(count, group, SEQ, D)

    def forward(weights, stream, cond):
        for index in range(LAYERS):
            stream = ref_block(stream, cond, [weight[index] for weight in weights])
        return stream

    def accumulate(totals, batch):
        stream, cond, back = batch
        result, pullback = jax.vjp(forward, params, stream, cond)
        grads, grad_stream, grad_cond = pullback(back)
        totals = tuple((total + grad for total, grad in zip(totals, grads)))
        return (totals, (result.astype(jnp.bfloat16), grad_stream, grad_cond))
    zeros = tuple((jnp.zeros_like(param) for param in params))
    totals, (results, grad_streams, grad_conds) = lax.scan(accumulate, zeros, (streams, conds, backs))
    squares = jnp.float32(0.0)
    for total in totals:
        squares = squares + jnp.sum(total * total)
    grad_norm = jnp.sqrt(squares)
    factor = jnp.minimum(1.0, clip_scale * math.sqrt(PARAMS) / grad_norm)
    news, next_firsts, next_seconds = ([], [], [])
    for index in range(6):
        decay = 0.0 if index == 1 else weight_decay
        new, first_new, second_new = adam_step(params[index], firsts[index], seconds[index], totals[index], factor, decay, learn_rates[index])
        news.append(new)
        next_firsts.append(first_new)
        next_seconds.append(second_new)
    return (results.reshape(LATENTS, SEQ, D), grad_streams.reshape(LATENTS, SEQ, D), grad_conds.reshape(LATENTS, D), news[0], news[1], news[2], news[3], news[4], news[5], next_firsts[0], next_firsts[1], next_firsts[2], next_firsts[3], next_firsts[4], next_firsts[5], next_seconds[0], next_seconds[1], next_seconds[2], next_seconds[3], next_seconds[4], next_seconds[5], grad_norm)
```

```python
import math

import jax
import jax.numpy as jnp
from jax import lax
from jax.sharding import PartitionSpec as P

HEAD_DIM = 64
LAYERS = 2
MICRO = 2
STEP = 10
PARAMS = 21242880


norm_epsilon = 1e-06
first_decay = 0.9
second_decay = 0.95
learn_rates = (0.03, 1.0, 0.03, 0.1, 0.03, 0.03)
weight_decay = 0.1
adam_epsilon = 1e-08
clip_scale = 0.5
highest = lax.Precision.HIGHEST


def modulate(stream, shift, scale):
    center = jnp.mean(stream, -1, keepdims=True)
    centred = stream - center
    spread = jnp.mean(centred * centred, -1, keepdims=True)
    return centred * lax.rsqrt(spread + norm_epsilon) * (1.0 + scale) + shift


def gelu_tanh(value):
    return jax.nn.gelu(value, approximate=True)


def layer_forward(stream, modul, weights):
    w_qkv, w_proj, w_fc1, w_fc2 = weights
    batch, length, width = stream.shape
    heads = width // HEAD_DIM
    scaling = HEAD_DIM ** (-0.5)
    normed = modulate(stream, modul[:, 0, None, :], modul[:, 1, None, :]).astype(jnp.bfloat16)
    qkv = jnp.dot(normed.reshape(batch * length, width), w_qkv, preferred_element_type=jnp.float32)
    qkv = qkv.astype(jnp.bfloat16).reshape(batch, length, 3, heads, HEAD_DIM)
    query = qkv[:, :, 0]
    keys = qkv[:, :, 1]
    values = qkv[:, :, 2]
    scores = (
        jnp.einsum("bqhe,bkhe->bhqk", query, keys, preferred_element_type=jnp.float32) * scaling
    )
    peak = jnp.max(scores, -1, keepdims=True)
    expo = jnp.exp(scores - peak)
    totals = jnp.sum(expo, -1, keepdims=True)
    probs = (expo / totals).astype(jnp.bfloat16)
    logsum = peak + jnp.log(totals)
    attended = jnp.einsum("bhqk,bkhe->bqhe", probs, values, preferred_element_type=jnp.float32)
    attended = attended.reshape(batch * length, width).astype(jnp.bfloat16)
    branch = jnp.dot(attended, w_proj, preferred_element_type=jnp.float32).reshape(
        batch, length, width
    )
    middle = stream + modul[:, 2, None, :] * branch
    normed_two = modulate(middle, modul[:, 3, None, :], modul[:, 4, None, :]).astype(jnp.bfloat16)
    upper = jnp.dot(
        normed_two.reshape(batch * length, width), w_fc1, preferred_element_type=jnp.float32
    )
    active = gelu_tanh(upper).astype(jnp.bfloat16)
    mlp_out = jnp.dot(active, w_fc2, preferred_element_type=jnp.float32).reshape(
        batch, length, width
    )
    result = middle + modul[:, 5, None, :] * mlp_out
    kept = (
        stream,
        modul,
        normed,
        query,
        keys,
        values,
        logsum,
        attended,
        branch,
        middle,
        normed_two,
        upper,
        active,
        mlp_out,
    )
    return (result, kept)


def layer_backward(grad_out, kept, weights):
    w_qkv, w_proj, w_fc1, w_fc2 = weights
    (
        stream,
        modul,
        normed,
        query,
        keys,
        values,
        logsum,
        attended,
        branch,
        middle,
        normed_two,
        upper,
        active,
        mlp_out,
    ) = kept
    batch, length, width = stream.shape
    heads = width // HEAD_DIM
    scaling = HEAD_DIM ** (-0.5)
    rows = batch * length
    d_gate2 = jnp.sum(grad_out * mlp_out, 1)
    d_mlp = (grad_out * modul[:, 5, None, :]).astype(jnp.bfloat16).reshape(rows, width)
    grad_fc2 = jnp.einsum("tf,td->fd", active, d_mlp, preferred_element_type=jnp.float32)
    d_active = jnp.einsum("td,fd->tf", d_mlp, w_fc2, preferred_element_type=jnp.float32)
    unused, gelu_back = jax.vjp(gelu_tanh, upper)
    d_upper = gelu_back(d_active)[0].astype(jnp.bfloat16)
    grad_fc1 = jnp.einsum(
        "td,tf->df", normed_two.reshape(rows, width), d_upper, preferred_element_type=jnp.float32
    )
    d_normed_two = jnp.einsum(
        "tf,df->td", d_upper, w_fc1, preferred_element_type=jnp.float32
    ).reshape(batch, length, width)
    unused, mod_back_two = jax.vjp(modulate, middle, modul[:, 3, None, :], modul[:, 4, None, :])
    d_middle_ln, d_shift2, d_scale2 = mod_back_two(d_normed_two)
    d_middle = grad_out + d_middle_ln
    d_gate1 = jnp.sum(d_middle * branch, 1)
    d_branch = (d_middle * modul[:, 2, None, :]).astype(jnp.bfloat16).reshape(rows, width)
    grad_proj = jnp.einsum("td,te->de", attended, d_branch, preferred_element_type=jnp.float32)
    d_attended = jnp.einsum("te,de->td", d_branch, w_proj, preferred_element_type=jnp.float32)
    d_attended = d_attended.astype(jnp.bfloat16).reshape(batch, length, heads, HEAD_DIM)
    scores = (
        jnp.einsum("bqhe,bkhe->bhqk", query, keys, preferred_element_type=jnp.float32) * scaling
    )
    probs = jnp.exp(scores - logsum)
    probs_low = probs.astype(jnp.bfloat16)
    d_values = jnp.einsum(
        "bhqk,bqhe->bkhe", probs_low, d_attended, preferred_element_type=jnp.float32
    )
    d_probs = jnp.einsum("bqhe,bkhe->bhqk", d_attended, values, preferred_element_type=jnp.float32)
    d_scores = (probs * (d_probs - jnp.sum(d_probs * probs, -1, keepdims=True))).astype(
        jnp.bfloat16
    )
    d_query = (
        jnp.einsum("bhqk,bkhe->bqhe", d_scores, keys, preferred_element_type=jnp.float32) * scaling
    )
    d_keys = (
        jnp.einsum("bhqk,bqhe->bkhe", d_scores, query, preferred_element_type=jnp.float32) * scaling
    )
    d_qkv = (
        jnp.stack([d_query, d_keys, d_values], axis=2).astype(jnp.bfloat16).reshape(rows, 3 * width)
    )
    grad_qkv = jnp.einsum(
        "td,te->de", normed.reshape(rows, width), d_qkv, preferred_element_type=jnp.float32
    )
    d_normed = jnp.einsum("te,de->td", d_qkv, w_qkv, preferred_element_type=jnp.float32).reshape(
        batch, length, width
    )
    unused, mod_back_one = jax.vjp(modulate, stream, modul[:, 0, None, :], modul[:, 1, None, :])
    d_stream_ln, d_shift1, d_scale1 = mod_back_one(d_normed)
    d_stream = d_middle + d_stream_ln
    d_modul = jnp.stack(
        [d_shift1[:, 0], d_scale1[:, 0], d_gate1, d_shift2[:, 0], d_scale2[:, 0], d_gate2], axis=1
    )
    return (d_stream, d_modul, (grad_qkv, grad_proj, grad_fc1, grad_fc2))


def adam_step(weight, first, second, grad, factor, decay, rate):
    grad = grad * factor
    first_new = first_decay * first + (1.0 - first_decay) * grad
    second_new = second_decay * second + (1.0 - second_decay) * grad * grad
    ratio = (
        first_new
        / (1.0 - first_decay**STEP)
        / (jnp.sqrt(second_new / (1.0 - second_decay**STEP)) + adam_epsilon)
    )
    return (weight - rate * (ratio + decay * weight), first_new, second_new)


def swap(value, axis, bit):
    return lax.ppermute(value, axis, [(i, i ^ bit) for i in range(lax.axis_size(axis))])


def gather_bits(value, axis):
    held = value[None]
    bit = 1
    while bit < lax.axis_size(axis):
        other = swap(held, axis, bit)
        high = (lax.axis_index(axis) // bit) % 2 == 1
        held = jnp.where(
            high, jnp.concatenate([other, held]), jnp.concatenate([held, other])
        )
        bit *= 2
    return held


def scatter_bits(value, axis):
    bit = 1
    while bit < lax.axis_size(axis):
        halves = value.reshape((value.shape[0] // 2, 2) + value.shape[1:])
        high = (lax.axis_index(axis) // bit) % 2 == 1
        keep = jnp.where(high, halves[:, 1], halves[:, 0])
        send = jnp.where(high, halves[:, 0], halves[:, 1])
        value = keep + swap(send, axis, bit)
        bit *= 2
    return value[0]


def to_blocks(piece, count):
    rows, columns = piece.shape
    width = columns // count
    return piece.reshape(rows, count, width).transpose(1, 0, 2).reshape(count * rows, width)


def local(tokens, condition, cotangent, *states):
    masters, firsts, seconds = (states[0:6], states[6:12], states[12:18])
    w_ada, b_ada, w_qkv, w_proj, w_fc1, w_fc2 = masters
    owners = lax.axis_size("shard")
    replicas = lax.axis_size("rep")
    me = lax.axis_index("shard")
    batch, length, width = tokens.shape
    part = w_qkv.shape[1]
    low = [weight.astype(jnp.bfloat16) for weight in (w_qkv, w_proj, w_fc1, w_fc2)]
    counts = (3, 1, 4)

    weights = []
    for index in range(LAYERS):
        blocks = [to_blocks(low[kind][index], counts[kind]) for kind in range(3)]
        packed = jnp.concatenate(blocks + [low[3][index]], 0)
        full = lax.all_gather(packed, "shard", axis=0)
        place = 0
        taken = []
        for kind in range(3):
            rows = counts[kind] * part
            block = full[:, place : place + rows].reshape(owners, counts[kind], part, width)
            taken.append(
                block.transpose(0, 2, 1, 3).reshape(owners * part, counts[kind] * width)
            )
            place += rows
        taken.append(full[:, place:].reshape(-1, width))
        weights.append(taken)

    cond_act = jax.nn.silu(condition).astype(jnp.bfloat16)
    cond_rep = gather_bits(cond_act, "shard")
    cond_all = gather_bits(cond_rep, "rep")
    cond_mine = lax.dynamic_slice_in_dim(cond_rep, me * part, part, 2).reshape(-1, part)
    cond_mine_all = lax.dynamic_slice_in_dim(cond_all, me * part, part, 3).reshape(-1, part)
    ada_low = w_ada.astype(jnp.bfloat16)
    bias_low = b_ada.astype(jnp.bfloat16).astype(jnp.float32)
    shares = []
    for index in range(LAYERS):
        share = jnp.dot(cond_mine, ada_low[index], preferred_element_type=jnp.float32)
        bias = lax.dynamic_update_slice(
            jnp.zeros((6, width), jnp.float32), bias_low[index], (0, me * part)
        )
        shares.append(share.reshape(owners, batch, 6, width) + bias)
    modul_all = scatter_bits(jnp.stack(shares, 2), "shard")

    stream = tokens.astype(jnp.float32)
    kept_all = []
    for index in range(LAYERS):
        stream, kept = layer_forward(stream, modul_all[:, index], weights[index])
        kept_all.append(kept)
    result = stream.astype(jnp.bfloat16)
    grad_stream = cotangent.astype(jnp.float32)
    owned = [None] * LAYERS
    grad_ada, grad_bias = ([None] * LAYERS, [None] * LAYERS)
    d_cond = jnp.zeros((owners * batch, part), jnp.float32)
    for index in reversed(range(LAYERS)):
        grad_stream, d_modul, grads = layer_backward(grad_stream, kept_all[index], weights[index])
        packs = [
            grads[kind]
            .astype(jnp.bfloat16)
            .reshape(owners, part, counts[kind], width)
            .transpose(0, 2, 1, 3)
            .reshape(owners, counts[kind] * part, width)
            for kind in range(3)
        ]
        packs.append(grads[3].astype(jnp.bfloat16).reshape(owners, -1, width))
        packed = jnp.concatenate(packs, 1)
        rows = packed.shape[1]
        split = packed.reshape(owners, replicas, rows // replicas, width).transpose(1, 0, 2, 3)
        mine = lax.psum_scatter(split.reshape(replicas * owners, -1, width), ("rep", "shard"), scatter_dimension=0)
        owned[index] = gather_bits(mine, "rep").reshape(rows, width).astype(jnp.float32)
        flat = d_modul.astype(jnp.bfloat16).reshape(batch, 6 * width)
        flat_rep = gather_bits(flat, "shard")
        flat_all = gather_bits(flat_rep, "rep").reshape(-1, 6 * width)
        grad_ada[index] = jnp.einsum("bd,bj->dj", cond_mine_all, flat_all, preferred_element_type=jnp.float32)
        totals = jnp.sum(flat_all.astype(jnp.float32), 0).reshape(6, width)
        grad_bias[index] = lax.dynamic_slice_in_dim(totals, me * part, part, 1)
        d_cond = d_cond + jnp.einsum(
            "bj,dj->bd", flat_rep.reshape(-1, 6 * width), ada_low[index], preferred_element_type=jnp.float32
        )
    d_cond_all = gather_bits(d_cond, "shard")
    d_cond_mine = lax.dynamic_slice_in_dim(d_cond_all, me * batch, batch, 1)
    grad_cond_act = d_cond_mine.transpose(1, 0, 2).reshape(batch, width)
    unused, silu_back = jax.vjp(jax.nn.silu, condition)
    grad_condition = silu_back(grad_cond_act)[0]

    def kind_of(packed, kind):
        place = part * sum(counts[:kind])
        if kind == 3:
            return packed[place:]
        rows = counts[kind] * part
        block = packed[place : place + rows].reshape(counts[kind], part, width)
        return block.transpose(1, 0, 2).reshape(part, counts[kind] * width)

    reduced = [jnp.stack(grad_ada), jnp.stack(grad_bias)] + [
        jnp.stack([kind_of(owned[index], kind) for index in range(LAYERS)]) for kind in range(4)
    ]
    squares = jnp.float32(0.0)
    for grad in reduced:
        squares = squares + jnp.sum(grad * grad)
    bit = 1
    while bit < owners:
        squares = squares + swap(squares, "shard", bit)
        bit *= 2
    grad_norm = jnp.sqrt(squares)
    factor = jnp.minimum(1.0, clip_scale * math.sqrt(PARAMS) / grad_norm)
    news, next_firsts, next_seconds = ([], [], [])
    for kind in range(6):
        decay = 0.0 if kind == 1 else weight_decay
        new, first_new, second_new = adam_step(
            masters[kind],
            firsts[kind],
            seconds[kind],
            reduced[kind],
            factor,
            decay,
            learn_rates[kind],
        )
        news.append(new)
        next_firsts.append(first_new)
        next_seconds.append(second_new)
    return (result, grad_stream, grad_condition, *news, *next_firsts, *next_seconds, grad_norm)


def solution(mesh):
    in_specs = (
        P(("rep", "shard"), None, None),
        P(("rep", "shard"), None),
        P(("rep", "shard"), None, None),
        P(None, "shard", None),
        P(None, None, "shard"),
        P(None, "shard", None),
        P(None, "shard", None),
        P(None, "shard", None),
        P(None, "shard", None),
        P(None, "shard", None),
        P(None, None, "shard"),
        P(None, "shard", None),
        P(None, "shard", None),
        P(None, "shard", None),
        P(None, "shard", None),
        P(None, "shard", None),
        P(None, None, "shard"),
        P(None, "shard", None),
        P(None, "shard", None),
        P(None, "shard", None),
        P(None, "shard", None),
    )
    out_specs = (
        P(("rep", "shard"), None, None),
        P(("rep", "shard"), None, None),
        P(("rep", "shard"), None),
        P(None, "shard", None),
        P(None, None, "shard"),
        P(None, "shard", None),
        P(None, "shard", None),
        P(None, "shard", None),
        P(None, "shard", None),
        P(None, "shard", None),
        P(None, None, "shard"),
        P(None, "shard", None),
        P(None, "shard", None),
        P(None, "shard", None),
        P(None, "shard", None),
        P(None, "shard", None),
        P(None, None, "shard"),
        P(None, "shard", None),
        P(None, "shard", None),
        P(None, "shard", None),
        P(None, "shard", None),
        P(),
    )
    return jax.shard_map(local, mesh=mesh, in_specs=in_specs, out_specs=out_specs, check_vma=False)
```

```python
import functools
import math

import jax
import jax.numpy as jnp
from jax import lax
from jax.experimental import pallas as pl
from jax.experimental.pallas import tpu as pltpu
from jax.sharding import PartitionSpec as P

HEAD_DIM = 64
LAYERS = 2
STEP = 10
PARAMS = 21242880
BLOCK = 768
VMEM_LIMIT = 56 * 1024 * 1024

norm_epsilon = 1e-06
first_decay = 0.9
second_decay = 0.95
learn_rates = (0.03, 1.0, 0.03, 0.1, 0.03, 0.03)
weight_decay = 0.1
adam_epsilon = 1e-08
clip_scale = 0.5

f32 = jnp.float32
bf16 = jnp.bfloat16


def dot_nn(left, right):
    return lax.dot_general(left, right, (((1,), (0,)), ((), ())), preferred_element_type=f32)


def dot_nt(left, right):
    return lax.dot_general(left, right, (((1,), (1,)), ((), ())), preferred_element_type=f32)


def dot_tn(left, right):
    return lax.dot_general(left, right, (((0,), (0,)), ((), ())), preferred_element_type=f32)


def relative(place):
    return 4 * (place & 1) + 8 * ((place >> 1) & 1) + 2 * (place >> 2)


def load_weights(here, pieces, held, sem):
    if len(pieces) == 1:
        pltpu.make_async_copy(pieces[0], held, sem).start()
    else:
        parts = len(pieces) // 2
        for number, piece in enumerate(pieces):
            core, turn = number // parts, number % parts
            places, rows, width = piece.shape
            column = pl.multiple_of((here[1] ^ turn) * width, 128) if parts > 1 else 0
            for place in range(places):
                owner = here[0] ^ (relative(place) + core)
                row = pl.multiple_of(owner * rows, rows)
                pltpu.make_async_copy(
                    piece.at[place], held.at[pl.ds(row, rows), pl.ds(column, width)], sem
                ).start()
    return pltpu.make_async_copy(held, held, sem).wait


def store_grads(here, grads, outs, sems, column):
    if len(outs) == 1:
        pltpu.make_async_copy(
            grads.at[:, pl.ds(column, BLOCK)], outs[0].at[:, pl.ds(column, BLOCK)], sems.at[0]
        ).start()
        return
    parts, places, rows, width = outs[0].shape
    turn = (column // width) ^ here[1] if parts > 1 else 0
    inner = pl.multiple_of(lax.rem(column, width), 128) if parts > 1 else column
    for core in range(2):
        for place in range(places):
            owner = here[0] ^ (relative(place) + core)
            row = pl.multiple_of(owner * rows, rows)
            pltpu.make_async_copy(
                grads.at[pl.ds(row, rows), pl.ds(column, BLOCK)],
                outs[core].at[turn, place, :, pl.ds(inner, BLOCK)],
                sems.at[core],
            ).start()


def wait_grads(outs, sems):
    for number, out in enumerate(outs):
        pltpu.make_async_copy(out, out, sems.at[number]).wait()


def normalise(value):
    centred = value - jnp.mean(value, -1, keepdims=True)
    spread = jnp.mean(centred * centred, -1, keepdims=True)
    rate = lax.rsqrt(spread + norm_epsilon)
    return centred * rate, rate


def normalise_back(grad, value, scale):
    unit, rate = normalise(value)
    d_shift = jnp.sum(grad, 0, keepdims=True)
    d_scale = jnp.sum(grad * unit, 0, keepdims=True)
    inner = grad * (1.0 + scale)
    d_value = rate * (
        inner
        - jnp.mean(inner, -1, keepdims=True)
        - unit * jnp.mean(inner * unit, -1, keepdims=True)
    )
    return d_value, d_shift, d_scale


def head_masks(rows):
    lane = lax.broadcasted_iota(jnp.int32, (rows, 2 * HEAD_DIM), 1)
    return lane < HEAD_DIM, lane >= HEAD_DIM


def pick(mask, value):
    return jnp.where(mask, value, jnp.zeros_like(value))


def attention_forward(count, here, x, mod, *refs):
    pieces, (xm, qkv, o, a, x1), (held, sem) = refs[:count], refs[count : count + 5], refs[count + 5 :]
    wait = load_weights(here, pieces, held, sem)
    latents, length, width = x.shape

    @pl.loop(0, latents)
    def _(lat):
        unit, _ = normalise(x[lat].astype(f32))
        xm[lat] = (unit * (1.0 + mod[lat, 1:2, :]) + mod[lat, 0:1, :]).astype(bf16)

    wait()

    @pl.loop(0, latents)
    def _(lat):
        @pl.loop(0, 3)
        def _(block):
            columns = pl.ds(pl.multiple_of(block * width, 128), width)
            qkv[lat, :, columns] = dot_nn(xm[lat], held[:, columns]).astype(bf16)

        @pl.loop(0, width // (2 * HEAD_DIM))
        def _(pair):
            lanes = 2 * HEAD_DIM
            start = pl.multiple_of(pair * lanes, lanes)
            query = qkv[lat, :, pl.ds(start, lanes)] * bf16(HEAD_DIM**-0.5)
            keys = qkv[lat, :, pl.ds(width + start, lanes)]
            values = qkv[lat, :, pl.ds(2 * width + start, lanes)]
            total = jnp.zeros((length, lanes), f32)
            for mask in head_masks(length):
                scores = dot_nt(pick(mask, query), keys)
                expo = jnp.exp(scores - jnp.max(scores, -1, keepdims=True))
                probs = (expo * (1.0 / jnp.sum(expo, -1, keepdims=True))).astype(bf16)
                total = total + dot_nn(probs, pick(mask, values))
            o[lat, :, pl.ds(start, lanes)] = total.astype(bf16)

        branch = dot_nn(o[lat], held[:, 3 * width : 4 * width])
        a[lat] = branch.astype(bf16)
        x1[lat] = x[lat].astype(f32) + mod[lat, 2:3, :] * branch


def gelu_parts(value):
    c = math.sqrt(2.0 / math.pi)
    square = value * value
    tanh = jnp.tanh(c * value * (1.0 + 0.044715 * square))
    half = 0.5 * (1.0 + tanh)
    slope = half + 0.5 * value * (1.0 - tanh * tanh) * c * (1.0 + 3.0 * 0.044715 * square)
    return value * half, slope


def feed_forward(count, here, x1, mod, *refs):
    pieces, (xm2, u, m, x2), (held, total, sem) = refs[:count], refs[count : count + 4], refs[count + 4 :]
    wait = load_weights(here, pieces, held, sem)
    latents, length, width = x1.shape
    blocks = held.shape[1] // width // 2

    @pl.loop(0, latents)
    def _(lat):
        unit, _ = normalise(x1[lat])
        xm2[lat] = (unit * (1.0 + mod[lat, 4:5, :]) + mod[lat, 3:4, :]).astype(bf16)

    wait()

    @pl.loop(0, latents)
    def _(lat):
        total[...] = jnp.zeros_like(total)

        @pl.loop(0, blocks)
        def _(block):
            columns = pl.ds(pl.multiple_of(block * width, 128), width)
            lower = pl.ds(pl.multiple_of((blocks + block) * width, 128), width)
            upper = dot_nn(xm2[lat], held[:, columns])
            u[lat, :, columns] = upper.astype(bf16)
            active = gelu_parts(upper)[0].astype(bf16)
            total[...] += dot_nn(active, held[:, lower])

        m[lat] = total[...].astype(bf16)
        x2[lat] = x1[lat] + mod[lat, 5:6, :] * total[...]


def feed_forward_back(count, given, here, d2, x1, mod, xm2, u, m, *refs):
    pieces, refs = refs[:count], refs[count:]
    d1, dmod = refs[:2]
    outs, refs = refs[2 : 2 + given], refs[2 + given :]
    held, grads, dm, active, du, total, sem, sems = refs
    wait = load_weights(here, pieces, held, sem)
    latents, length, width = x1.shape
    blocks = held.shape[1] // width // 2

    @pl.loop(0, latents)
    def _(lat):
        rows = pl.ds(pl.multiple_of(lat * length, length), length)
        grad = d2[lat].astype(f32)
        dmod[lat, 2:3, :] = jnp.sum(grad * m[lat].astype(f32), 0, keepdims=True)
        dm[rows, :] = (grad * mod[lat, 5:6, :]).astype(bf16)

    wait()
    total[...] = jnp.zeros_like(total)

    @pl.loop(0, blocks)
    def _(block):
        left = pl.multiple_of(block * width, 128)
        right = pl.multiple_of((blocks + block) * width, 128)

        @pl.loop(0, latents)
        def _(lat):
            rows = pl.ds(pl.multiple_of(lat * length, length), length)
            value, slope = gelu_parts(u[lat, :, pl.ds(left, width)].astype(f32))
            active[rows, :] = value.astype(bf16)
            d_active = dot_nt(dm[rows, :], held[:, pl.ds(right, width)])
            du[rows, :] = (d_active * slope).astype(bf16)
            total[rows, :] += dot_nt(du[rows, :], held[:, pl.ds(left, width)])

        @pl.loop(0, width // 256)
        def _(step):
            rows = pl.ds(pl.multiple_of(step * 256, 256), 256)
            grads[rows, pl.ds(right, width)] = dot_tn(active[:, rows], dm[...]).astype(bf16)
            grads[rows, pl.ds(left, width)] = dot_tn(
                xm2[:, :, rows].reshape(latents * length, 256), du[...]
            ).astype(bf16)

        store_grads(here, grads, outs, sems, left)
        store_grads(here, grads, outs, sems, right)

    @pl.loop(0, latents)
    def _(lat):
        rows = pl.ds(pl.multiple_of(lat * length, length), length)
        back, d_shift, d_scale = normalise_back(total[rows, :], x1[lat], mod[lat, 4:5, :])
        dmod[lat, 0:1, :] = d_shift
        dmod[lat, 1:2, :] = d_scale
        d1[lat] = d2[lat].astype(f32) + back

    wait_grads(outs, sems)


def attention_back(count, given, here, d1, x, mod, xm, qkv, o, a, *refs):
    pieces, refs = refs[:count], refs[count:]
    d0, dmod = refs[:2]
    outs, refs = refs[2 : 2 + given], refs[2 + given :]
    held, grads, da, do, dqkv, sem, sems = refs
    wait = load_weights(here, pieces, held, sem)
    latents, length, width = x.shape
    lanes = 2 * HEAD_DIM

    @pl.loop(0, latents)
    def _(lat):
        rows = pl.ds(pl.multiple_of(lat * length, length), length)
        grad = d1[lat]
        dmod[lat, 2:3, :] = jnp.sum(grad * a[lat].astype(f32), 0, keepdims=True)
        da[rows, :] = (grad * mod[lat, 2:3, :]).astype(bf16)

    wait()

    @pl.loop(0, width // 256)
    def _(step):
        rows = pl.ds(pl.multiple_of(step * 256, 256), 256)
        grads[rows, 3 * width : 4 * width] = dot_tn(
            o[:, :, rows].reshape(latents * length, 256), da[...]
        ).astype(bf16)

    store_grads(here, grads, outs, sems, 3 * width)

    @pl.loop(0, latents)
    def _(lat):
        rows = pl.ds(pl.multiple_of(lat * length, length), length)
        do[...] = dot_nt(da[rows, :], held[:, 3 * width : 4 * width]).astype(bf16)

        @pl.loop(0, width // lanes)
        def _(pair):
            start = pl.multiple_of(pair * lanes, lanes)
            query = qkv[lat, :, pl.ds(start, lanes)] * bf16(HEAD_DIM**-0.5)
            keys = qkv[lat, :, pl.ds(width + start, lanes)]
            values = qkv[lat, :, pl.ds(2 * width + start, lanes)]
            d_out = do[:, pl.ds(start, lanes)]
            d_query = jnp.zeros((length, lanes), f32)
            d_keys = jnp.zeros((length, lanes), f32)
            d_values = jnp.zeros((length, lanes), f32)
            for mask in head_masks(length):
                own_query, own_out = pick(mask, query), pick(mask, d_out)
                scores = dot_nt(keys, own_query)
                expo = jnp.exp(scores - jnp.max(scores, 0, keepdims=True))
                probs = expo * (1.0 / jnp.sum(expo, 0, keepdims=True))
                d_values = d_values + dot_nn(probs.astype(bf16), own_out)
                d_probs = dot_nt(values, own_out)
                inner = jnp.sum(d_probs * probs, 0, keepdims=True)
                d_scores = (probs * (d_probs - inner)).astype(bf16)
                d_keys = d_keys + dot_nn(d_scores, own_query)
                d_query = d_query + dot_tn(d_scores, pick(mask, keys))
            dqkv[rows, pl.ds(start, lanes)] = (d_query * HEAD_DIM**-0.5).astype(bf16)
            dqkv[rows, pl.ds(width + start, lanes)] = d_keys.astype(bf16)
            dqkv[rows, pl.ds(2 * width + start, lanes)] = d_values.astype(bf16)

    @pl.loop(0, 3)
    def _(block):
        left = pl.multiple_of(block * width, 128)

        @pl.loop(0, width // 256)
        def _(step):
            rows = pl.ds(pl.multiple_of(step * 256, 256), 256)
            grads[rows, pl.ds(left, width)] = dot_tn(
                xm[:, :, rows].reshape(latents * length, 256), dqkv[:, pl.ds(left, width)]
            ).astype(bf16)

        store_grads(here, grads, outs, sems, left)

    @pl.loop(0, latents)
    def _(lat):
        rows = pl.ds(pl.multiple_of(lat * length, length), length)
        total = dot_nt(dqkv[rows, :], held[:, : 3 * width])
        back, d_shift, d_scale = normalise_back(total, x[lat].astype(f32), mod[lat, 1:2, :])
        dmod[lat, 0:1, :] = d_shift
        dmod[lat, 1:2, :] = d_scale
        d0[lat] = d1[lat] + back

    wait_grads(outs, sems)


def kernel_call(body, here, arrays, pieces, outs, package_outs, scratch, flops):
    vmem = pl.BlockSpec(memory_space=pltpu.VMEM)
    anywhere = pl.BlockSpec(memory_space=pl.ANY)
    moved = sum(v.size * v.dtype.itemsize for v in list(arrays) + list(pieces) + list(outs) + list(package_outs))
    return pl.pallas_call(
        body,
        in_specs=[pl.BlockSpec(memory_space=pltpu.SMEM)] + [vmem] * len(arrays) + [anywhere] * len(pieces),
        out_specs=[vmem] * len(outs) + [anywhere] * len(package_outs),
        out_shape=list(outs) + list(package_outs),
        scratch_shapes=scratch,
        compiler_params=pltpu.CompilerParams(vmem_limit_bytes=VMEM_LIMIT),
        cost_estimate=pl.CostEstimate(flops=flops, bytes_accessed=moved, transcendentals=0),
    )(here, *arrays, *pieces)


def shaped(shape, dtype):
    return jax.ShapeDtypeStruct(shape, dtype)


def call_attention(here, x, mod, pieces):
    latents, length, width = x.shape
    tokens = latents * length
    like = lambda columns, dtype: shaped((latents, length, columns), dtype)
    return kernel_call(
        functools.partial(attention_forward, len(pieces)),
        here,
        (x, mod),
        pieces,
        (like(width, bf16), like(3 * width, bf16), like(width, bf16), like(width, bf16), like(width, f32)),
        (),
        [pltpu.VMEM((width, 4 * width), bf16), pltpu.SemaphoreType.DMA],
        2 * tokens * width * 4 * width + 8 * tokens * length * width,
    )


def call_feed_forward(here, x1, mod, pieces, columns):
    latents, length, width = x1.shape
    like = lambda count, dtype: shaped((latents, length, count), dtype)
    return kernel_call(
        functools.partial(feed_forward, len(pieces)),
        here,
        (x1, mod),
        pieces,
        (like(width, bf16), like(columns // 2, bf16), like(width, bf16), like(width, f32)),
        (),
        [pltpu.VMEM((width, columns), bf16), pltpu.VMEM((length, width), f32), pltpu.SemaphoreType.DMA],
        2 * latents * length * width * columns,
    )


def call_feed_forward_back(here, d2, x1, mod, xm2, u, m, pieces, package_outs, columns):
    latents, length, width = x1.shape
    tokens = latents * length
    return kernel_call(
        functools.partial(feed_forward_back, len(pieces), len(package_outs)),
        here,
        (d2, x1, mod, xm2, u, m),
        pieces,
        (shaped(x1.shape, f32), shaped((latents, 3, width), f32)),
        package_outs,
        [
            pltpu.VMEM((width, columns), bf16),
            pltpu.VMEM((width, columns), bf16),
            pltpu.VMEM((tokens, width), bf16),
            pltpu.VMEM((tokens, width), bf16),
            pltpu.VMEM((tokens, width), bf16),
            pltpu.VMEM((tokens, width), f32),
            pltpu.SemaphoreType.DMA,
            pltpu.SemaphoreType.DMA((2,)),
        ],
        4 * tokens * width * columns,
    )


def call_attention_back(here, d1, x, mod, xm, qkv, o, a, pieces, package_outs):
    latents, length, width = x.shape
    tokens = latents * length
    return kernel_call(
        functools.partial(attention_back, len(pieces), len(package_outs)),
        here,
        (d1, x, mod, xm, qkv, o, a),
        pieces,
        (shaped(x.shape, f32), shaped((latents, 3, width), f32)),
        package_outs,
        [
            pltpu.VMEM((width, 4 * width), bf16),
            pltpu.VMEM((width, 4 * width), bf16),
            pltpu.VMEM((tokens, width), bf16),
            pltpu.VMEM((length, width), bf16),
            pltpu.VMEM((tokens, 3 * width), bf16),
            pltpu.SemaphoreType.DMA,
            pltpu.SemaphoreType.DMA((2,)),
        ],
        16 * tokens * width * width + 40 * tokens * length * width,
    )


def swap(value, axis, bit):
    return lax.ppermute(value, axis, [(i, i ^ bit) for i in range(lax.axis_size(axis))])


def gather_bits(value, axis):
    held = value[None]
    bit = 1
    while bit < lax.axis_size(axis):
        other = swap(held, axis, bit)
        high = (lax.axis_index(axis) // bit) % 2 == 1
        held = jnp.where(high, jnp.concatenate([other, held]), jnp.concatenate([held, other]))
        bit *= 2
    return held


def scatter_bits(value, axis):
    bit = 1
    while bit < lax.axis_size(axis):
        halves = value.reshape((value.shape[0] // 2, 2) + value.shape[1:])
        high = (lax.axis_index(axis) // bit) % 2 == 1
        keep = jnp.where(high, halves[:, 1], halves[:, 0])
        send = jnp.where(high, halves[:, 0], halves[:, 1])
        value = keep + swap(send, axis, bit)
        bit *= 2
    return value[0]


def sum_bits(value, axis):
    bit = 1
    while bit < lax.axis_size(axis):
        value = value + swap(value, axis, bit)
        bit *= 2
    return value


def gather_package(piece, split, by_place):
    if not by_place:
        full = gather_bits(piece, "shard")
        return [full.reshape(-1, piece.shape[1])]
    if split:
        width = piece.shape[1] // 2
        piece = lax.dynamic_slice_in_dim(piece, lax.axis_index("rep") * width, width, 1)
    held = piece[None]
    for bit in (4, 8, 2):
        held = jnp.concatenate([held, swap(held, "shard", bit)])
    groups = [held] + ([swap(held, "rep", 1)] if split else [])
    return groups + [swap(group, "shard", 1) for group in groups]


def package_shapes(rows, columns, split, by_place):
    if not by_place:
        return (shaped((BLOCK, columns), bf16),)
    parts = 2 if split else 1
    return (shaped((parts, 8, rows, columns // parts), bf16),) * 2


def scatter_package(package, split, by_place):
    if not by_place:
        owners = lax.axis_size("shard")
        full = package[0].reshape(owners, -1, package[0].shape[1])
        return sum_bits(scatter_bits(full, "shard").astype(f32), "rep")
    keep, send = package
    held = keep + swap(send, "shard", 1)
    held = held[0] + swap(held[1], "rep", 1) if split else held[0]
    for half, bit in ((4, 2), (2, 8), (1, 4)):
        held = held[:half] + swap(held[half:], "shard", bit)
    held = held[0]
    other = swap(held, "rep", 1)
    if not split:
        return held.astype(f32) + other.astype(f32)
    ordered = jnp.where(
        lax.axis_index("rep") == 0,
        jnp.concatenate([held, other], 1),
        jnp.concatenate([other, held], 1),
    )
    return ordered.astype(f32)


def adam_step(weight, first, second, grad, factor, decay, rate):
    grad = grad * factor
    first_new = first_decay * first + (1.0 - first_decay) * grad
    second_new = second_decay * second + (1.0 - second_decay) * grad * grad
    ratio = (
        first_new
        / (1.0 - first_decay**STEP)
        / (jnp.sqrt(second_new / (1.0 - second_decay**STEP)) + adam_epsilon)
    )
    return (weight - rate * (ratio + decay * weight), first_new, second_new)


def local(tokens, condition, cotangent, *states):
    masters, firsts, seconds = (states[0:6], states[6:12], states[12:18])
    w_ada, b_ada, w_qkv, w_proj, w_fc1, w_fc2 = masters
    owners = lax.axis_size("shard")
    replicas = lax.axis_size("rep")
    me = lax.axis_index("shard")
    here = jnp.stack([me, lax.axis_index("rep")]).astype(jnp.int32)
    batch, length, width = tokens.shape
    part = w_qkv.shape[1]
    groups = w_fc2.shape[1] // part
    by_place = owners == 16 and replicas == 2
    split_attention, split_feed = False, True
    feed_columns = w_fc1.shape[2] + groups * width

    def fc1_out(value):
        return value.reshape(part, owners, groups, part).transpose(0, 2, 1, 3).reshape(part, -1)

    def fc1_back(value):
        return value.reshape(part, groups, owners, part).transpose(0, 2, 1, 3).reshape(part, -1)

    def fc2_out(value):
        return value.reshape(groups, part, width).transpose(1, 0, 2).reshape(part, -1)

    def fc2_back(value):
        return value.reshape(part, groups, width).transpose(1, 0, 2).reshape(-1, width)

    attention_weights, feed_weights = [], []
    for index in range(LAYERS):
        piece = jnp.concatenate([w_qkv[index], w_proj[index]], 1).astype(bf16)
        attention_weights.append(gather_package(piece, split_attention, by_place))
        piece = jnp.concatenate([fc1_out(w_fc1[index].astype(bf16)), fc2_out(w_fc2[index].astype(bf16))], 1)
        feed_weights.append(gather_package(piece, split_feed, by_place))

    cond_act = jax.nn.silu(condition).astype(bf16)
    cond_rep = gather_bits(cond_act, "shard")
    cond_all = gather_bits(cond_rep, "rep")
    cond_mine = lax.dynamic_slice_in_dim(cond_rep, me * part, part, 2).reshape(-1, part)
    cond_mine_all = lax.dynamic_slice_in_dim(cond_all, me * part, part, 3).reshape(-1, part)
    ada_low = w_ada.astype(bf16)
    bias_low = b_ada.astype(bf16).astype(f32)
    shares = []
    for index in range(LAYERS):
        share = jnp.dot(cond_mine, ada_low[index], preferred_element_type=f32)
        bias = lax.dynamic_update_slice(jnp.zeros((6, width), f32), bias_low[index], (0, me * part))
        shares.append(share.reshape(owners, batch, 6, width) + bias)
    modul = scatter_bits(jnp.stack(shares, 2), "shard")

    stream = tokens
    kept = []
    for index in range(LAYERS):
        mod = modul[:, index]
        xm, qkv, o, a, x1 = call_attention(here, stream, mod, attention_weights[index])
        xm2, u, m, x2 = call_feed_forward(here, x1, mod, feed_weights[index], feed_columns)
        kept.append((stream, mod, xm, qkv, o, a, x1, xm2, u, m))
        stream = x2
    result = stream.astype(bf16)

    grad_stream = cotangent
    owned = [None] * LAYERS
    grad_ada, grad_bias = ([None] * LAYERS, [None] * LAYERS)
    d_cond = jnp.zeros((owners * batch, part), f32)
    for index in reversed(range(LAYERS)):
        x, mod, xm, qkv, o, a, x1, xm2, u, m = kept[index]
        d1, dmod_two, *package = call_feed_forward_back(
            here, grad_stream, x1, mod, xm2, u, m, feed_weights[index],
            package_shapes(part, feed_columns, split_feed, by_place), feed_columns,
        )
        feed_grad = scatter_package(package, split_feed, by_place)
        grad_stream, dmod_one, *package = call_attention_back(
            here, d1, x, mod, xm, qkv, o, a, attention_weights[index],
            package_shapes(part, 4 * width, split_attention, by_place),
        )
        attention_grad = scatter_package(package, split_attention, by_place)
        hidden = w_fc1.shape[2]
        owned[index] = (
            attention_grad[:, : 3 * width],
            attention_grad[:, 3 * width :],
            fc1_back(feed_grad[:, :hidden]),
            fc2_back(feed_grad[:, hidden:]),
        )
        flat = jnp.concatenate([dmod_one, dmod_two], 1).astype(bf16).reshape(batch, 6 * width)
        flat_rep = gather_bits(flat, "shard")
        flat_all = gather_bits(flat_rep, "rep").reshape(-1, 6 * width)
        grad_ada[index] = jnp.einsum("bd,bj->dj", cond_mine_all, flat_all, preferred_element_type=f32)
        totals = jnp.sum(flat_all.astype(f32), 0).reshape(6, width)
        grad_bias[index] = lax.dynamic_slice_in_dim(totals, me * part, part, 1)
        d_cond = d_cond + jnp.einsum(
            "bj,dj->bd", flat_rep.reshape(-1, 6 * width), ada_low[index], preferred_element_type=f32
        )
    d_cond_all = gather_bits(d_cond, "shard")
    d_cond_mine = lax.dynamic_slice_in_dim(d_cond_all, me * batch, batch, 1)
    grad_cond_act = d_cond_mine.transpose(1, 0, 2).reshape(batch, width)
    unused, silu_back = jax.vjp(jax.nn.silu, condition)
    grad_condition = silu_back(grad_cond_act)[0]

    reduced = [jnp.stack(grad_ada), jnp.stack(grad_bias)] + [
        jnp.stack([owned[index][kind] for index in range(LAYERS)]) for kind in range(4)
    ]
    squares = jnp.float32(0.0)
    for grad in reduced:
        squares = squares + jnp.sum(grad * grad)
    grad_norm = jnp.sqrt(sum_bits(squares, "shard"))
    factor = jnp.minimum(1.0, clip_scale * math.sqrt(PARAMS) / grad_norm)
    news, next_firsts, next_seconds = ([], [], [])
    for kind in range(6):
        new, first_new, second_new = adam_step(
            masters[kind],
            firsts[kind],
            seconds[kind],
            reduced[kind],
            factor,
            0.0 if kind == 1 else weight_decay,
            learn_rates[kind],
        )
        news.append(new)
        next_firsts.append(first_new)
        next_seconds.append(second_new)
    return (result, grad_stream, grad_condition, *news, *next_firsts, *next_seconds, grad_norm)


def solution(mesh):
    latents = P(("rep", "shard"), None, None)
    weights = (P(None, "shard", None), P(None, None, "shard")) + (P(None, "shard", None),) * 4
    in_specs = (latents, P(("rep", "shard"), None), latents) + weights * 3
    out_specs = (latents, latents, P(("rep", "shard"), None)) + weights * 3 + (P(),)
    return jax.shard_map(local, mesh=mesh, in_specs=in_specs, out_specs=out_specs, check_vma=False)
```

```python
import functools
import math

import jax
import jax.numpy as jnp
from jax import lax
from jax.experimental import pallas as pl
from jax.experimental.pallas import tpu as pltpu
from jax.sharding import PartitionSpec as P

HEAD_DIM = 64
LAYERS = 2
STEP = 10
PARAMS = 21242880
FC_UNITS = 4
LAYER_UNITS = 12
PROJ, FC1, FC2 = 3, 4, 8
VMEM_LIMIT = 56 * 1024 * 1024

norm_epsilon = 1e-06
first_decay = 0.9
second_decay = 0.95
learn_rates = (0.03, 1.0, 0.03, 0.1, 0.03, 0.03)
weight_decay = 0.1
adam_epsilon = 1e-08
clip_scale = 0.5

f32 = jnp.float32
bf16 = jnp.bfloat16


def dot_nn(left, right):
    return lax.dot_general(left, right, (((1,), (0,)), ((), ())), preferred_element_type=f32)


def dot_nt(left, right):
    return lax.dot_general(left, right, (((1,), (1,)), ((), ())), preferred_element_type=f32)


def dot_tn(left, right):
    return lax.dot_general(left, right, (((0,), (0,)), ((), ())), preferred_element_type=f32)


def relative(place):
    return 4 * (place & 1) + 8 * ((place >> 1) & 1) + 2 * (place >> 2)


def matrix(block):
    rows, width = block.shape[-2:]
    if rows % 16 == 0:
        return block.reshape(-1, width)
    return block.astype(f32).reshape(-1, width).astype(block.dtype)


def load_weights(packed, first, held, sem):
    copy = pltpu.make_async_copy(packed.at[:, pl.ds(first, held.shape[1])], held, sem)
    copy.start()
    return copy.wait


def store_grads(here, grads, outs, sems, unit, units, first=0, number=None):
    number = grads.shape[0] if number is None else number
    chosen = pl.ds(unit, units)
    if len(outs) == 1:
        owners = pl.ds(first, number)
        pltpu.make_async_copy(
            grads.at[owners, chosen], outs[0].at[owners, chosen], sems.at[0]
        ).start()
        return
    parts, places, _, _, width = outs[0].shape
    for step in range(number):
        owner = first + step
        other = owner ^ here[0]
        place = 4 * ((other >> 1) & 1) + 2 * ((other >> 3) & 1) + ((other >> 2) & 1)
        for core in range(2):

            @pl.when((other & 1) == core)
            def _():
                for turn in range(parts):
                    column = pl.multiple_of((turn ^ here[1]) * width, 128) if parts > 1 else 0
                    pltpu.make_async_copy(
                        grads.at[owner, chosen, :, pl.ds(column, width)],
                        outs[core].at[turn, place, chosen],
                        sems.at[core],
                    ).start()


def wait_grads(outs, sems):
    for number, out in enumerate(outs):
        pltpu.make_async_copy(out, out, sems.at[number]).wait()


def weight_grad(left, right, grads, unit):
    tokens, width = right.shape
    owners, _, rows, _ = grads.shape
    half = width // 2

    @pl.loop(0, 2)
    def _(step):
        columns = pl.ds(pl.multiple_of(step * half, 128), half)
        product = dot_tn(left(columns), right)
        grads[pl.ds(step * (owners // 2), owners // 2), unit] = product.reshape(
            owners // 2, rows, width
        ).astype(bf16)


def pack_weights(qkv, proj, fc1, fc2, packed):
    rows, width = packed.shape[1:]
    for layer in range(qkv.shape[0]):
        base = layer * LAYER_UNITS
        for unit in range(PROJ):
            packed[base + unit] = qkv[layer, :, unit * width : (unit + 1) * width].astype(bf16)
        packed[base + PROJ] = proj[layer].astype(bf16)
        for unit in range(FC_UNITS):
            packed[base + FC1 + unit] = fc1[layer, :, unit * width : (unit + 1) * width].astype(bf16)
            packed[base + FC2 + unit] = fc2[layer, unit * rows : (unit + 1) * rows].astype(bf16)


def normalise(value):
    centred = value - jnp.mean(value, -1, keepdims=True)
    spread = jnp.mean(centred * centred, -1, keepdims=True)
    rate = lax.rsqrt(spread + norm_epsilon)
    return centred * rate, rate


def normalise_back(grad, value, scale):
    unit, rate = normalise(value)
    d_shift = jnp.sum(grad, 0, keepdims=True)
    d_scale = jnp.sum(grad * unit, 0, keepdims=True)
    inner = grad * (1.0 + scale)
    d_value = rate * (
        inner
        - jnp.mean(inner, -1, keepdims=True)
        - unit * jnp.mean(inner * unit, -1, keepdims=True)
    )
    return d_value, d_shift, d_scale


def head_masks(rows):
    lane = lax.broadcasted_iota(jnp.int32, (rows, 2 * HEAD_DIM), 1)
    return lane < HEAD_DIM, lane >= HEAD_DIM


def pick(mask, value):
    return jnp.where(mask, value, jnp.zeros_like(value))


def attention_forward(base, x, mod, packed, xm, qkv, o, a, x1, held, sem):
    wait = load_weights(packed, base, held, sem)
    latents, length, width = x.shape

    @pl.loop(0, latents)
    def _(lat):
        unit, _ = normalise(x[lat].astype(f32))
        xm[lat] = (unit * (1.0 + mod[lat, 1:2, :]) + mod[lat, 0:1, :]).astype(bf16)

    wait()

    @pl.loop(0, latents)
    def _(lat):
        @pl.loop(0, 3)
        def _(block):
            columns = pl.ds(pl.multiple_of(block * width, 128), width)
            qkv[lat, :, columns] = dot_nn(xm[lat], matrix(held[:, block])).astype(bf16)

        @pl.loop(0, width // (2 * HEAD_DIM))
        def _(pair):
            lanes = 2 * HEAD_DIM
            start = pl.multiple_of(pair * lanes, lanes)
            query = qkv[lat, :, pl.ds(start, lanes)] * bf16(HEAD_DIM**-0.5)
            keys = qkv[lat, :, pl.ds(width + start, lanes)]
            values = qkv[lat, :, pl.ds(2 * width + start, lanes)]
            total = jnp.zeros((length, lanes), f32)
            for mask in head_masks(length):
                scores = dot_nt(pick(mask, query), keys)
                expo = jnp.exp(scores - jnp.max(scores, -1, keepdims=True))
                probs = (expo * (1.0 / jnp.sum(expo, -1, keepdims=True))).astype(bf16)
                total = total + dot_nn(probs, pick(mask, values))
            o[lat, :, pl.ds(start, lanes)] = total.astype(bf16)

        branch = dot_nn(o[lat], matrix(held[:, PROJ]))
        a[lat] = branch.astype(bf16)
        x1[lat] = x[lat].astype(f32) + mod[lat, 2:3, :] * branch


def gelu_parts(value):
    c = math.sqrt(2.0 / math.pi)
    square = value * value
    tanh = jnp.tanh(c * value * (1.0 + 0.044715 * square))
    half = 0.5 * (1.0 + tanh)
    slope = half + 0.5 * value * (1.0 - tanh * tanh) * c * (1.0 + 3.0 * 0.044715 * square)
    return value * half, slope


def feed_forward(base, x1, mod, packed, xm2, u, m, x2, held, total, sem):
    wait = load_weights(packed, base + FC1, held, sem)
    latents, length, width = x1.shape
    share = held.shape[0] // FC_UNITS

    @pl.loop(0, latents)
    def _(lat):
        unit, _ = normalise(x1[lat])
        xm2[lat] = (unit * (1.0 + mod[lat, 4:5, :]) + mod[lat, 3:4, :]).astype(bf16)

    wait()

    @pl.loop(0, latents)
    def _(lat):
        total[...] = jnp.zeros_like(total)

        @pl.loop(0, FC_UNITS)
        def _(block):
            columns = pl.ds(pl.multiple_of(block * width, 128), width)
            upper = dot_nn(xm2[lat], matrix(held[:, block]))
            u[lat, :, columns] = upper.astype(bf16)
            active = gelu_parts(upper)[0].astype(bf16)
            total[...] += dot_nn(active, matrix(held[pl.ds(block * share, share), FC_UNITS:]))

        m[lat] = total[...].astype(bf16)
        x2[lat] = x1[lat] + mod[lat, 5:6, :] * total[...]


def lower_back(base, given, here, d2, mod, u, m, packed, *refs):
    refs = refs[-(8 + given) :]
    du, dgate = refs[:2]
    outs, (held, grads, dm, active, sem, sems) = refs[2 : 2 + given], refs[2 + given :]
    wait = load_weights(packed, base + FC2, held, sem)
    latents, length, width = d2.shape
    tokens = latents * length
    owners, _, part, _ = held.shape
    share = owners // FC_UNITS

    @pl.loop(0, latents)
    def _(lat):
        rows = pl.ds(pl.multiple_of(lat * length, length), length)
        grad = d2[lat].astype(f32)
        dgate[lat] = jnp.sum(grad * m[lat].astype(f32), 0, keepdims=True)
        dm[rows, :] = (grad * mod[lat, 5:6, :]).astype(bf16)

    wait()

    @pl.loop(0, FC_UNITS)
    def _(block):
        columns = pl.ds(pl.multiple_of(block * width, 128), width)

        @pl.loop(0, latents)
        def _(lat):
            rows = pl.ds(pl.multiple_of(lat * length, length), length)
            value, slope = gelu_parts(u[lat, :, columns].astype(f32))
            active[rows, :] = value.astype(bf16)
            d_active = dot_nt(dm[rows, :], matrix(held[pl.ds(block * share, share)]))
            du[lat, :, columns] = (d_active * slope).astype(bf16)

        @pl.loop(0, 2)
        def _(step):
            half = pl.ds(pl.multiple_of(step * (width // 2), 128), width // 2)
            product = dot_tn(active[:, half], dm[...]).reshape(share // 2, FC_UNITS, part, width)
            grads[pl.ds(block * share + step * (share // 2), share // 2)] = product.astype(bf16)

        store_grads(here, grads, outs, sems, 0, FC_UNITS, block * share, share)

    wait_grads(outs, sems)


def upper_back(base, given, here, d2, x1, mod, xm2, du, o, a, packed, *refs):
    refs = refs[-(8 + given) :]
    d1, dmod, da = refs[:3]
    outs, (held, grads, total, sem, sems) = refs[3 : 3 + given], refs[3 + given : 8 + given]
    wait = load_weights(packed, base + FC1, held, sem)
    latents, length, width = x1.shape
    tokens = latents * length

    @pl.loop(0, FC_UNITS)
    def _(block):
        columns = pl.ds(pl.multiple_of(block * width, 128), width)
        weight_grad(
            lambda some: xm2[:, :, some].reshape(tokens, -1),
            du[:, :, columns].reshape(tokens, width),
            grads,
            block,
        )

    store_grads(here, grads, outs, sems, 0, FC_UNITS)
    wait()

    @pl.loop(0, latents)
    def _(lat):
        total[...] = jnp.zeros_like(total)

        @pl.loop(0, FC_UNITS)
        def _(block):
            columns = pl.ds(pl.multiple_of(block * width, 128), width)
            total[...] += dot_nt(du[lat, :, columns], matrix(held[:, block]))

        back, d_shift, d_scale = normalise_back(total[...], x1[lat], mod[lat, 4:5, :])
        grad = d2[lat].astype(f32) + back
        dmod[lat, 1:2, :] = d_shift
        dmod[lat, 2:3, :] = d_scale
        dmod[lat, 0:1, :] = jnp.sum(grad * a[lat].astype(f32), 0, keepdims=True)
        d1[lat] = grad
        da[lat] = (grad * mod[lat, 2:3, :]).astype(bf16)

    weight_grad(
        lambda some: o[:, :, some].reshape(tokens, -1), da[...].reshape(tokens, width), grads, FC_UNITS
    )
    store_grads(here, grads, outs, sems, FC_UNITS, 1)
    wait_grads(outs, sems)


def attention_back(base, given, here, d1, x, mod, xm, qkv, da, packed, *refs):
    refs = refs[-(8 + given) :]
    d0, dmod = refs[:2]
    outs, (held, grads, do, dqkv, sem, sems) = refs[2 : 2 + given], refs[2 + given :]
    wait = load_weights(packed, base, held, sem)
    latents, length, width = x.shape
    tokens = latents * length
    lanes = 2 * HEAD_DIM
    wait()

    @pl.loop(0, latents)
    def _(lat):
        rows = pl.ds(pl.multiple_of(lat * length, length), length)
        do[...] = dot_nt(da[lat], matrix(held[:, PROJ])).astype(bf16)

        @pl.loop(0, width // lanes)
        def _(pair):
            start = pl.multiple_of(pair * lanes, lanes)
            query = qkv[lat, :, pl.ds(start, lanes)] * bf16(HEAD_DIM**-0.5)
            keys = qkv[lat, :, pl.ds(width + start, lanes)]
            values = qkv[lat, :, pl.ds(2 * width + start, lanes)]
            d_out = do[:, pl.ds(start, lanes)]
            d_query = jnp.zeros((length, lanes), f32)
            d_keys = jnp.zeros((length, lanes), f32)
            d_values = jnp.zeros((length, lanes), f32)
            for mask in head_masks(length):
                own_query, own_out = pick(mask, query), pick(mask, d_out)
                scores = dot_nt(keys, own_query)
                expo = jnp.exp(scores - jnp.max(scores, 0, keepdims=True))
                probs = expo * (1.0 / jnp.sum(expo, 0, keepdims=True))
                d_values = d_values + dot_nn(probs.astype(bf16), own_out)
                d_probs = dot_nt(values, own_out)
                inner = jnp.sum(d_probs * probs, 0, keepdims=True)
                d_scores = (probs * (d_probs - inner)).astype(bf16)
                d_keys = d_keys + dot_nn(d_scores, own_query)
                d_query = d_query + dot_tn(d_scores, pick(mask, keys))
            dqkv[rows, pl.ds(start, lanes)] = (d_query * HEAD_DIM**-0.5).astype(bf16)
            dqkv[rows, pl.ds(width + start, lanes)] = d_keys.astype(bf16)
            dqkv[rows, pl.ds(2 * width + start, lanes)] = d_values.astype(bf16)

    @pl.loop(0, 3)
    def _(block):
        columns = pl.ds(pl.multiple_of(block * width, 128), width)
        weight_grad(
            lambda some: xm[:, :, some].reshape(tokens, -1), dqkv[:, columns], grads, block
        )

    store_grads(here, grads, outs, sems, 0, 3)

    @pl.loop(0, latents)
    def _(lat):
        rows = pl.ds(pl.multiple_of(lat * length, length), length)
        total = jnp.zeros((length, width), f32)
        for block in range(3):
            total = total + dot_nt(dqkv[rows, block * width : (block + 1) * width], matrix(held[:, block]))
        back, d_shift, d_scale = normalise_back(total, x[lat].astype(f32), mod[lat, 1:2, :])
        dmod[lat, 0:1, :] = d_shift
        dmod[lat, 1:2, :] = d_scale
        d0[lat] = d1[lat] + back

    wait_grads(outs, sems)


def update(units, factor, rate, weight, first, second, grad0, grad1, new, first_new, second_new):
    layer, unit = pl.program_id(0), pl.program_id(1)
    grad = jnp.where(layer == 0, grad0[units + unit], grad1[units + unit])
    results = adam_step(weight[0], first[0], second[0], grad, factor[0], weight_decay, rate)
    new[0], first_new[0], second_new[0] = results


def adam_step(weight, first, second, grad, factor, decay, rate):
    grad = grad * factor
    first_new = first_decay * first + (1.0 - first_decay) * grad
    second_new = second_decay * second + (1.0 - second_decay) * grad * grad
    ratio = (
        first_new
        / (1.0 - first_decay**STEP)
        / (jnp.sqrt(second_new / (1.0 - second_decay**STEP)) + adam_epsilon)
    )
    return (weight - rate * (ratio + decay * weight), first_new, second_new)


def kernel_call(body, scalars, arrays, others, outs, package_outs, scratch, flops):
    vmem = pl.BlockSpec(memory_space=pltpu.VMEM)
    anywhere = pl.BlockSpec(memory_space=pl.ANY)
    moved = sum(v.size * v.dtype.itemsize for v in list(arrays) + list(outs) + list(package_outs))
    return pl.pallas_call(
        body,
        in_specs=[pl.BlockSpec(memory_space=pltpu.SMEM)] * len(scalars)
        + [vmem] * len(arrays)
        + [anywhere] * len(others),
        out_specs=[vmem] * len(outs) + [anywhere] * len(package_outs),
        out_shape=list(outs) + list(package_outs),
        scratch_shapes=scratch,
        compiler_params=pltpu.CompilerParams(vmem_limit_bytes=VMEM_LIMIT),
        cost_estimate=pl.CostEstimate(flops=flops, bytes_accessed=moved, transcendentals=0),
    )(*scalars, *arrays, *others)


def shaped(shape, dtype):
    return jax.ShapeDtypeStruct(shape, dtype)


def call_pack(w_qkv, w_proj, w_fc1, w_fc2):
    layers, rows, width = w_proj.shape
    out = shaped((layers * LAYER_UNITS, rows, width), bf16)
    return kernel_call(pack_weights, (), (w_qkv, w_proj, w_fc1, w_fc2), (), (out,), (), [], 0)[0]


def call_attention(base, x, mod, packed):
    latents, length, width = x.shape
    tokens = latents * length
    owners, _, rows, _ = packed.shape
    like = lambda columns, dtype: shaped((latents, length, columns), dtype)
    return kernel_call(
        functools.partial(attention_forward, base),
        (),
        (x, mod),
        (packed,),
        (like(width, bf16), like(3 * width, bf16), like(width, bf16), like(width, bf16), like(width, f32)),
        (),
        [pltpu.VMEM((owners, 4, rows, width), bf16), pltpu.SemaphoreType.DMA],
        2 * tokens * width * 4 * width + 8 * tokens * length * width,
    )


def call_feed_forward(base, x1, mod, packed):
    latents, length, width = x1.shape
    owners, _, rows, _ = packed.shape
    like = lambda count, dtype: shaped((latents, length, count), dtype)
    return kernel_call(
        functools.partial(feed_forward, base),
        (),
        (x1, mod),
        (packed,),
        (like(width, bf16), like(FC_UNITS * width, bf16), like(width, bf16), like(width, f32)),
        (),
        [
            pltpu.VMEM((owners, 2 * FC_UNITS, rows, width), bf16),
            pltpu.VMEM((length, width), f32),
            pltpu.SemaphoreType.DMA,
        ],
        2 * latents * length * width * 2 * FC_UNITS * width,
    )


def call_back(body, base, here, arrays, packed, after, outs, package_outs, held_units, units, scratch, flops):
    owners, _, rows, width = packed.shape
    return kernel_call(
        functools.partial(body, base, len(package_outs)),
        (here,),
        arrays,
        (packed, *after),
        outs,
        package_outs,
        [pltpu.VMEM((owners, held_units, rows, width), bf16), pltpu.VMEM((owners, units, rows, width), bf16)]
        + scratch
        + [pltpu.SemaphoreType.DMA, pltpu.SemaphoreType.DMA((2,))],
        flops,
    )


def call_lower_back(base, here, d2, mod, u, m, packed, after, package_outs):
    latents, length, width = d2.shape
    tokens = latents * length
    return call_back(
        lower_back, base, here, (d2, mod, u, m), packed, after,
        (shaped(u.shape, bf16), shaped((latents, 1, width), f32)), package_outs,
        FC_UNITS, FC_UNITS,
        [pltpu.VMEM((tokens, width), bf16), pltpu.VMEM((tokens, width), bf16)],
        4 * tokens * width * FC_UNITS * width,
    )


def call_upper_back(base, here, d2, x1, mod, xm2, du, o, a, packed, after, package_outs):
    latents, length, width = x1.shape
    return call_back(
        upper_back, base, here, (d2, x1, mod, xm2, du, o, a), packed, after,
        (shaped(x1.shape, f32), shaped((latents, 3, width), f32), shaped(x1.shape, bf16)), package_outs,
        FC_UNITS, FC_UNITS + 1,
        [pltpu.VMEM((length, width), f32)],
        4 * latents * length * width * FC_UNITS * width,
    )


def call_attention_back(base, here, d1, x, mod, xm, qkv, da, packed, after, package_outs):
    latents, length, width = x.shape
    tokens = latents * length
    return call_back(
        attention_back, base, here, (d1, x, mod, xm, qkv, da), packed, after,
        (shaped(x.shape, f32), shaped((latents, 2, width), f32)), package_outs,
        4, 3,
        [pltpu.VMEM((length, width), bf16), pltpu.VMEM((tokens, 3 * width), bf16)],
        14 * tokens * width * width + 40 * tokens * length * width,
    )


def call_update(first_unit, by_rows, rate, factor, weight, first, second, grad0, grad1):
    rows, width = grad0.shape[1:]
    units = weight.shape[1] * weight.shape[2] // (rows * width)
    place = (lambda layer, unit: (layer, unit, 0)) if by_rows else (lambda layer, unit: (layer, 0, unit))
    block = pl.BlockSpec((1, rows, width), place)
    whole = pl.BlockSpec(memory_space=pltpu.VMEM)
    return pl.pallas_call(
        lambda factor_ref, *refs: update(first_unit, factor_ref, rate, *refs),
        grid=(weight.shape[0], units),
        in_specs=[pl.BlockSpec(memory_space=pltpu.SMEM), block, block, block, whole, whole],
        out_specs=[block] * 3,
        out_shape=[shaped(weight.shape, f32)] * 3,
        compiler_params=pltpu.CompilerParams(vmem_limit_bytes=VMEM_LIMIT),
    )(factor, weight, first, second, grad0, grad1)


def swap(value, axis, bit):
    return lax.ppermute(value, axis, [(i, i ^ bit) for i in range(lax.axis_size(axis))])


def gather_bits(value, axis):
    held = value[None]
    bit = 1
    while bit < lax.axis_size(axis):
        other = swap(held, axis, bit)
        high = (lax.axis_index(axis) // bit) % 2 == 1
        held = jnp.where(high, jnp.concatenate([other, held]), jnp.concatenate([held, other]))
        bit *= 2
    return held


def scatter_bits(value, axis):
    bit = 1
    while bit < lax.axis_size(axis):
        halves = value.reshape((value.shape[0] // 2, 2) + value.shape[1:])
        high = (lax.axis_index(axis) // bit) % 2 == 1
        keep = jnp.where(high, halves[:, 1], halves[:, 0])
        send = jnp.where(high, halves[:, 0], halves[:, 1])
        value = keep + swap(send, axis, bit)
        bit *= 2
    return value[0]


def sum_bits(value, axis):
    bit = 1
    while bit < lax.axis_size(axis):
        value = value + swap(value, axis, bit)
        bit *= 2
    return value


class Package:
    def __init__(self, arrays, split, by_place):
        self.arrays, self.split, self.by_place = arrays, split, by_place
        self.steps = ["core"] + (["rep"] if split else []) + [2, 8, 4, "end"] if by_place else []
        self.held = None

    def step(self):
        if not self.steps:
            return
        kind = self.steps.pop(0)
        if kind == "core":
            keep, send = self.arrays
            self.held = keep + swap(send, "shard", 1)
            if not self.split:
                self.held = self.held[0]
        elif kind == "rep":
            self.held = self.held[0] + swap(self.held[1], "rep", 1)
        elif kind == "end":
            held = self.held[0]
            other = swap(held, "rep", 1)
            if self.split:
                first = lax.axis_index("rep") == 0
                self.held = jnp.concatenate(
                    [jnp.where(first, held, other), jnp.where(first, other, held)], 2
                ).astype(f32)
            else:
                self.held = held.astype(f32) + other.astype(f32)
        else:
            half = self.held.shape[0] // 2
            self.held = self.held[:half] + swap(self.held[half:], "shard", kind)

    def finish(self):
        while self.steps:
            self.step()
        if not self.by_place:
            self.held = sum_bits(scatter_bits(self.arrays[0], "shard").astype(f32), "rep")
        return self.held


def package_shapes(packed, units, split, by_place):
    owners, _, rows, width = packed.shape
    if not by_place:
        return (shaped((owners, units, rows, width), bf16),)
    parts = 2 if split else 1
    return (shaped((parts, 8, units, rows, width // parts), bf16),) * 2


def local(tokens, condition, cotangent, *states):
    masters, firsts, seconds = (states[0:6], states[6:12], states[12:18])
    w_ada, b_ada, w_qkv, w_proj, w_fc1, w_fc2 = masters
    owners = lax.axis_size("shard")
    replicas = lax.axis_size("rep")
    me = lax.axis_index("shard")
    here = jnp.stack([me, lax.axis_index("rep")]).astype(jnp.int32)
    batch, length, width = tokens.shape
    part = w_qkv.shape[1]
    by_place = owners == 16 and replicas == 2

    packed = lax.all_gather(call_pack(w_qkv, w_proj, w_fc1, w_fc2), "shard", axis=0)

    cond_act = jax.nn.silu(condition).astype(bf16)
    cond_rep = gather_bits(cond_act, "shard")
    cond_all = gather_bits(cond_rep, "rep")
    cond_mine = lax.dynamic_slice_in_dim(cond_rep, me * part, part, 2).reshape(-1, part)
    cond_mine_all = lax.dynamic_slice_in_dim(cond_all, me * part, part, 3).reshape(-1, part)
    ada_low = w_ada.astype(bf16)
    bias_low = b_ada.astype(bf16).astype(f32)
    shares = []
    for index in range(LAYERS):
        share = jnp.dot(cond_mine, ada_low[index], preferred_element_type=f32)
        bias = lax.dynamic_update_slice(jnp.zeros((6, width), f32), bias_low[index], (0, me * part))
        shares.append(share.reshape(owners, batch, 6, width) + bias)
    modul = scatter_bits(jnp.stack(shares, 2), "shard")

    stream = tokens
    kept = []
    for index in range(LAYERS):
        mod = modul[:, index]
        base = index * LAYER_UNITS
        xm, qkv, o, a, x1 = call_attention(base, stream, mod, packed)
        xm2, u, m, x2 = call_feed_forward(base, x1, mod, packed)
        kept.append((stream, mod, xm, qkv, o, a, x1, xm2, u, m))
        stream = x2
    result = stream.astype(bf16)

    grad = cotangent
    lower, upper, attention = ([None] * LAYERS, [None] * LAYERS, [None] * LAYERS)
    d_modul = [None] * LAYERS
    moving = []

    def advance():
        for package in moving:
            package.step()
        return [package.held for package in moving if package.held is not None]

    def outgoing(units, split):
        return package_shapes(packed, units, split, by_place)

    after = []
    for index in reversed(range(LAYERS)):
        x, mod, xm, qkv, o, a, x1, xm2, u, m = kept[index]
        base = index * LAYER_UNITS
        split = False
        du, d_gate, *arrays = call_lower_back(
            base, here, grad, mod, u, m, packed, after, outgoing(FC_UNITS, split)
        )
        after = advance()
        lower[index] = Package(arrays, split, by_place)
        moving.append(lower[index])
        split = True
        d1, d_middle, da, *arrays = call_upper_back(
            base, here, grad, x1, mod, xm2, du, o, a, packed, after, outgoing(FC_UNITS + 1, split)
        )
        after = advance()
        upper[index] = Package(arrays, split, by_place)
        moving.append(upper[index])
        split = index == 0
        grad, d_first, *arrays = call_attention_back(
            base, here, d1, x, mod, xm, qkv, da, packed, after, outgoing(3, split)
        )
        after = advance()
        attention[index] = Package(arrays, split, by_place)
        moving.append(attention[index])
        d_modul[index] = jnp.concatenate([d_first, d_middle, d_gate], 1)

    flat = jnp.stack(d_modul, 1).astype(bf16).reshape(batch, LAYERS, 6 * width)
    flat_rep = gather_bits(flat, "shard")
    flat_all = gather_bits(flat_rep, "rep").reshape(-1, LAYERS, 6 * width)
    grad_ada = jnp.einsum("bd,blj->ldj", cond_mine_all, flat_all, preferred_element_type=f32)
    totals = jnp.sum(flat_all.astype(f32), 0).reshape(LAYERS, 6, width)
    grad_bias = lax.dynamic_slice_in_dim(totals, me * part, part, 2)
    d_cond = jnp.einsum(
        "blj,ldj->bd", flat_rep.reshape(-1, LAYERS, 6 * width), ada_low, preferred_element_type=f32
    )
    d_cond_all = gather_bits(d_cond, "shard")
    d_cond_mine = lax.dynamic_slice_in_dim(d_cond_all, me * batch, batch, 1)
    grad_cond_act = d_cond_mine.transpose(1, 0, 2).reshape(batch, width)
    unused, silu_back = jax.vjp(jax.nn.silu, condition)
    grad_condition = silu_back(grad_cond_act)[0]

    for package in moving:
        package.finish()
    squares = jnp.float32(0.0)
    for array in [grad_ada, grad_bias] + [package.held for package in moving]:
        squares = squares + jnp.sum(array * array)
    grad_norm = jnp.sqrt(sum_bits(squares, "shard"))
    factor = jnp.minimum(1.0, clip_scale * math.sqrt(PARAMS) / grad_norm)
    updated = []
    for kind, array in ((0, grad_ada), (1, grad_bias)):
        updated.append(
            adam_step(
                masters[kind],
                firsts[kind],
                seconds[kind],
                array,
                factor,
                0.0 if kind == 1 else weight_decay,
                learn_rates[kind],
            )
        )
    for kind, packages, first_unit in ((2, attention, 0), (3, upper, FC_UNITS), (4, upper, 0), (5, lower, 0)):
        updated.append(
            call_update(
                first_unit,
                kind == 5,
                learn_rates[kind],
                factor.reshape(1),
                masters[kind],
                firsts[kind],
                seconds[kind],
                packages[0].held,
                packages[1].held,
            )
        )
    news, next_firsts, next_seconds = zip(*updated)
    return (result, grad, grad_condition, *news, *next_firsts, *next_seconds, grad_norm)


def solution(mesh):
    latents = P(("rep", "shard"), None, None)
    weights = (P(None, "shard", None), P(None, None, "shard")) + (P(None, "shard", None),) * 4
    in_specs = (latents, P(("rep", "shard"), None), latents) + weights * 3
    out_specs = (latents, latents, P(("rep", "shard"), None)) + weights * 3 + (P(),)
    return jax.shard_map(local, mesh=mesh, in_specs=in_specs, out_specs=out_specs, check_vma=False)
```

```python
import functools
import math

import jax
import jax.numpy as jnp
from jax import lax
from jax.experimental import pallas as pl
from jax.experimental.pallas import tpu as pltpu
from jax.sharding import PartitionSpec as P

HEAD_DIM = 64
LAYERS = 2
STEP = 10
PARAMS = 21242880
FC_UNITS = 4
LAYER_UNITS = 12
PROJ, FC1, FC2 = 3, 4, 8
VMEM_LIMIT = 56 * 1024 * 1024

norm_epsilon = 1e-06
first_decay = 0.9
second_decay = 0.95
learn_rates = (0.03, 1.0, 0.03, 0.1, 0.03, 0.03)
weight_decay = 0.1
adam_epsilon = 1e-08
clip_scale = 0.5

f32 = jnp.float32
bf16 = jnp.bfloat16


def dot_nn(left, right):
    return lax.dot_general(left, right, (((1,), (0,)), ((), ())), preferred_element_type=f32)


def dot_nt(left, right):
    return lax.dot_general(left, right, (((1,), (1,)), ((), ())), preferred_element_type=f32)


def dot_tn(left, right):
    return lax.dot_general(left, right, (((0,), (0,)), ((), ())), preferred_element_type=f32)


def matrix(block):
    rows, width = block.shape[-2:]
    if rows % 16 == 0:
        return block.reshape(-1, width)
    return block.astype(f32).reshape(-1, width).astype(block.dtype)


def load_weights(packed, first, held, sem):
    copy = pltpu.make_async_copy(packed.at[:, pl.ds(first, held.shape[1])], held, sem)
    copy.start()
    return copy.wait


def store_grads(here, grads, outs, sems, unit, units, first=0, number=None, offset=0):
    number = grads.shape[0] if number is None else number
    chosen = pl.ds(unit, units)
    if len(outs) == 1:
        owners = pl.ds(first, number)
        pltpu.make_async_copy(
            grads.at[owners, chosen], outs[0].at[owners, pl.ds(offset + unit, units)], sems.at[0]
        ).start()
        return
    parts, places, _, _, width = outs[0].shape
    for step in range(number):
        owner = first + step
        other = owner ^ here[0]
        place = 4 * ((other >> 1) & 1) + 2 * ((other >> 2) & 1) + ((other >> 3) & 1)
        for core in range(2):

            @pl.when((other & 1) == core)
            def _():
                for turn in range(parts):
                    column = pl.multiple_of((turn ^ here[1]) * width, 128) if parts > 1 else 0
                    pltpu.make_async_copy(
                        grads.at[owner, chosen, :, pl.ds(column, width)],
                        outs[core].at[turn, place, chosen],
                        sems.at[core],
                    ).start()


def wait_grads(outs, sems, units, offset=0):
    for number, out in enumerate(outs):
        if len(outs) == 1:
            out = out.at[:, pl.ds(offset, units)]
        pltpu.make_async_copy(out, out, sems.at[number]).wait()


def weight_grad(left, right, grads, unit):
    owners, _, rows, width = grads.shape
    grads[:, unit] = dot_tn(left, right).reshape(owners, rows, width).astype(bf16)


def flat(value):
    return value.reshape(-1, value.shape[-1])


def pack_weights(qkv, proj, fc1, fc2, packed):
    rows, width = packed.shape[1:]
    for layer in range(qkv.shape[0]):
        base = layer * LAYER_UNITS
        for unit in range(PROJ):
            packed[base + unit] = qkv[layer, :, unit * width : (unit + 1) * width].astype(bf16)
        packed[base + PROJ] = proj[layer].astype(bf16)
        for unit in range(FC_UNITS):
            packed[base + FC1 + unit] = fc1[layer, :, unit * width : (unit + 1) * width].astype(bf16)
            packed[base + FC2 + unit] = fc2[layer, unit * rows : (unit + 1) * rows].astype(bf16)


def normalise(value):
    centred = value - jnp.mean(value, -1, keepdims=True)
    spread = jnp.mean(centred * centred, -1, keepdims=True)
    rate = lax.rsqrt(spread + norm_epsilon)
    return centred * rate, rate


def normalise_back(grad, value, scale):
    unit, rate = normalise(value)
    d_shift = jnp.sum(grad, 0, keepdims=True)
    d_scale = jnp.sum(grad * unit, 0, keepdims=True)
    inner = grad * (1.0 + scale)
    d_value = rate * (
        inner
        - jnp.mean(inner, -1, keepdims=True)
        - unit * jnp.mean(inner * unit, -1, keepdims=True)
    )
    return d_value, d_shift, d_scale


def head_masks(rows):
    lane = lax.broadcasted_iota(jnp.int32, (rows, 2 * HEAD_DIM), 1)
    return lane < HEAD_DIM, lane >= HEAD_DIM


def pick(mask, value):
    return jnp.where(mask, value, jnp.zeros_like(value))


def attention_forward(base, x, mod, packed, xm, qkv, o, a, x1, held, sems):
    waits = [load_weights(packed, base + unit, held.at[:, pl.ds(unit, 1)], sems.at[unit]) for unit in range(4)]
    latents, length, width = x.shape

    @pl.loop(0, latents)
    def _(lat):
        unit, _ = normalise(x[lat].astype(f32))
        xm[lat] = (unit * (1.0 + mod[lat, 1:2, :]) + mod[lat, 0:1, :]).astype(bf16)

    for block in range(3):
        waits[block]()
        product = dot_nn(flat(xm[...]), matrix(held[:, block])).astype(bf16)
        qkv[:, :, block * width : (block + 1) * width] = product.reshape(latents, length, width)

    @pl.loop(0, latents)
    def _(lat):
        @pl.loop(0, width // (2 * HEAD_DIM))
        def _(pair):
            lanes = 2 * HEAD_DIM
            start = pl.multiple_of(pair * lanes, lanes)
            query = qkv[lat, :, pl.ds(start, lanes)] * bf16(HEAD_DIM**-0.5)
            keys = qkv[lat, :, pl.ds(width + start, lanes)]
            values = qkv[lat, :, pl.ds(2 * width + start, lanes)]
            total = jnp.zeros((length, lanes), f32)
            for mask in head_masks(length):
                scores = dot_nt(pick(mask, query), keys)
                expo = jnp.exp(scores - jnp.max(scores, -1, keepdims=True))
                probs = (expo * (1.0 / jnp.sum(expo, -1, keepdims=True))).astype(bf16)
                total = total + dot_nn(probs, pick(mask, values))
            o[lat, :, pl.ds(start, lanes)] = total.astype(bf16)

    waits[PROJ]()
    branch = dot_nn(flat(o[...]), matrix(held[:, PROJ])).reshape(latents, length, width)
    for lat in range(latents):
        a[lat] = branch[lat].astype(bf16)
        x1[lat] = x[lat].astype(f32) + mod[lat, 2:3, :] * branch[lat]


def gelu_parts(value):
    c = math.sqrt(2.0 / math.pi)
    square = value * value
    tanh = jnp.tanh(c * value * (1.0 + 0.044715 * square))
    half = 0.5 * (1.0 + tanh)
    slope = half + 0.5 * value * (1.0 - tanh * tanh) * c * (1.0 + 3.0 * 0.044715 * square)
    return value * half, slope


def load_feed_forward(packed, base, held, sems):
    share = held.shape[0] // FC_UNITS
    both = held.shape[1] > FC_UNITS
    for block in range(FC_UNITS):
        if both:
            load_weights(packed, base + FC1 + block, held.at[:, pl.ds(block, 1)], sems.at[block])
        owners = pl.ds(block * share, share)
        units = pl.ds(held.shape[1] - FC_UNITS, FC_UNITS)
        pltpu.make_async_copy(
            packed.at[owners, pl.ds(base + FC2, FC_UNITS)], held.at[owners, units], sems.at[FC_UNITS + block]
        ).start()

    def wait_upper(block):
        column = held.at[:, pl.ds(block, 1)]
        pltpu.make_async_copy(column, column, sems.at[block]).wait()

    def wait_lower(block):
        rows = held.at[pl.ds(block * share, share), pl.ds(held.shape[1] - FC_UNITS, FC_UNITS)]
        pltpu.make_async_copy(rows, rows, sems.at[FC_UNITS + block]).wait()

    return wait_upper, wait_lower


def feed_forward(base, x1, mod, packed, xm2, u, m, x2, held, total, sems):
    wait_upper, wait_lower = load_feed_forward(packed, base, held, sems)
    latents, length, width = x1.shape
    share = held.shape[0] // FC_UNITS

    @pl.loop(0, latents)
    def _(lat):
        unit, _ = normalise(x1[lat])
        xm2[lat] = (unit * (1.0 + mod[lat, 4:5, :]) + mod[lat, 3:4, :]).astype(bf16)

    total[...] = jnp.zeros_like(total)

    @pl.loop(0, FC_UNITS)
    def _(block):
        columns = pl.ds(pl.multiple_of(block * width, 128), width)
        wait_upper(block)
        upper = dot_nn(flat(xm2[...]), matrix(held[:, block]))
        u[:, :, columns] = upper.astype(bf16).reshape(latents, length, width)
        active = gelu_parts(upper)[0].astype(bf16)
        wait_lower(block)
        total[...] += dot_nn(active, matrix(held[pl.ds(block * share, share), FC_UNITS:]))

    for lat in range(latents):
        result = total[lat * length : (lat + 1) * length, :]
        m[lat] = result.astype(bf16)
        x2[lat] = x1[lat] + mod[lat, 5:6, :] * result


def lower_back(base, given, here, d2, mod, u, m, packed, *refs):
    refs = refs[-(8 + given) :]
    du, dgate = refs[:2]
    outs, (held, grads, dm, active, load_sems, sems) = refs[2 : 2 + given], refs[2 + given :]
    _, wait_lower = load_feed_forward(packed, base, held, load_sems)
    latents, length, width = d2.shape
    owners, _, part, _ = held.shape
    share = owners // FC_UNITS

    @pl.loop(0, latents)
    def _(lat):
        rows = pl.ds(pl.multiple_of(lat * length, length), length)
        grad = d2[lat].astype(f32)
        dgate[lat] = jnp.sum(grad * m[lat].astype(f32), 0, keepdims=True)
        dm[rows, :] = (grad * mod[lat, 5:6, :]).astype(bf16)

    @pl.loop(0, FC_UNITS)
    def _(block):
        columns = pl.ds(pl.multiple_of(block * width, 128), width)
        shards = pl.ds(block * share, share)
        wait_lower(block)
        d_active = dot_nt(dm[...], matrix(held[shards]))
        value, slope = gelu_parts(flat(u[:, :, columns]).astype(f32))
        active[...] = value.astype(bf16)
        du[:, :, columns] = (d_active * slope).astype(bf16).reshape(latents, length, width)
        grads[shards] = dot_tn(active[...], dm[...]).reshape(share, FC_UNITS, part, width).astype(bf16)
        store_grads(here, grads, outs, sems, 0, FC_UNITS, block * share, share)

    wait_grads(outs, sems, FC_UNITS)


def upper_back(base, given, here, d2, x1, mod, xm2, du, o, a, packed, *refs):
    refs = refs[-(8 + given) :]
    d1, dmod, da = refs[:3]
    outs, (held, grads, total, sem, sems) = refs[3 : 3 + given], refs[3 + given : 8 + given]
    wait = load_weights(packed, base + FC1, held, sem)
    latents, length, width = x1.shape
    tokens = latents * length

    @pl.loop(0, FC_UNITS)
    def _(block):
        columns = pl.ds(pl.multiple_of(block * width, 128), width)
        weight_grad(flat(xm2[...]), flat(du[:, :, columns]), grads, block)

    store_grads(here, grads, outs, sems, 0, FC_UNITS)
    wait()
    total[...] = jnp.zeros_like(total)

    @pl.loop(0, FC_UNITS)
    def _(block):
        columns = pl.ds(pl.multiple_of(block * width, 128), width)
        total[...] += dot_nt(flat(du[:, :, columns]), matrix(held[:, block]))

    @pl.loop(0, latents)
    def _(lat):
        rows = pl.ds(pl.multiple_of(lat * length, length), length)
        back, d_shift, d_scale = normalise_back(total[rows, :], x1[lat], mod[lat, 4:5, :])
        grad = d2[lat].astype(f32) + back
        dmod[lat, 1:2, :] = d_shift
        dmod[lat, 2:3, :] = d_scale
        dmod[lat, 0:1, :] = jnp.sum(grad * a[lat].astype(f32), 0, keepdims=True)
        d1[lat] = grad
        da[lat] = (grad * mod[lat, 2:3, :]).astype(bf16)

    weight_grad(flat(o[...]), flat(da[...]), grads, FC_UNITS)
    store_grads(here, grads, outs, sems, FC_UNITS, 1)
    wait_grads(outs, sems, FC_UNITS + 1)


def attention_back(offset, base, given, here, d1, x, mod, xm, qkv, da, packed, *refs):
    refs = refs[-(9 + given) :]
    d0, dmod = refs[:2]
    outs, (held, grads, do, dqkv, total, sem, sems) = refs[2 : 2 + given], refs[2 + given :]
    wait = load_weights(packed, base, held, sem)
    latents, length, width = x.shape
    tokens = latents * length
    lanes = 2 * HEAD_DIM
    wait()
    do[...] = dot_nt(flat(da[...]), matrix(held[:, PROJ])).astype(bf16)

    @pl.loop(0, latents)
    def _(lat):
        rows = pl.ds(pl.multiple_of(lat * length, length), length)

        @pl.loop(0, width // lanes)
        def _(pair):
            start = pl.multiple_of(pair * lanes, lanes)
            query = qkv[lat, :, pl.ds(start, lanes)] * bf16(HEAD_DIM**-0.5)
            keys = qkv[lat, :, pl.ds(width + start, lanes)]
            values = qkv[lat, :, pl.ds(2 * width + start, lanes)]
            d_out = do[rows, pl.ds(start, lanes)]
            d_query = jnp.zeros((length, lanes), f32)
            d_keys = jnp.zeros((length, lanes), f32)
            d_values = jnp.zeros((length, lanes), f32)
            for mask in head_masks(length):
                own_query, own_out = pick(mask, query), pick(mask, d_out)
                scores = dot_nt(keys, own_query)
                expo = jnp.exp(scores - jnp.max(scores, 0, keepdims=True))
                probs = expo * (1.0 / jnp.sum(expo, 0, keepdims=True))
                d_values = d_values + dot_nn(probs.astype(bf16), own_out)
                d_probs = dot_nt(values, own_out)
                inner = jnp.sum(d_probs * probs, 0, keepdims=True)
                d_scores = (probs * (d_probs - inner)).astype(bf16)
                d_keys = d_keys + dot_nn(d_scores, own_query)
                d_query = d_query + dot_tn(d_scores, pick(mask, keys))
            dqkv[rows, pl.ds(start, lanes)] = (d_query * HEAD_DIM**-0.5).astype(bf16)
            dqkv[rows, pl.ds(width + start, lanes)] = d_keys.astype(bf16)
            dqkv[rows, pl.ds(2 * width + start, lanes)] = d_values.astype(bf16)

    @pl.loop(0, 3)
    def _(block):
        columns = pl.ds(pl.multiple_of(block * width, 128), width)
        weight_grad(flat(xm[...]), dqkv[:, columns], grads, block)

    store_grads(here, grads, outs, sems, 0, 3, offset=offset)

    total[...] = jnp.zeros_like(total)

    @pl.loop(0, 3)
    def _(block):
        columns = pl.ds(pl.multiple_of(block * width, 128), width)
        total[...] += dot_nt(dqkv[:, columns], matrix(held[:, block]))

    @pl.loop(0, latents)
    def _(lat):
        rows = pl.ds(pl.multiple_of(lat * length, length), length)
        back, d_shift, d_scale = normalise_back(total[rows, :], x[lat].astype(f32), mod[lat, 1:2, :])
        dmod[lat, 0:1, :] = d_shift
        dmod[lat, 1:2, :] = d_scale
        d0[lat] = d1[lat] + back

    wait_grads(outs, sems, 3, offset)


def update(first_units, by_rows, rate, factor, weight, first, second, grad0, grad1, new, first_new, second_new):
    layer, step = pl.program_id(0), pl.program_id(1)
    rows, width = grad0.shape[1:]
    count = weight.shape[1] * weight.shape[2] // (rows * width)
    for number in range(count):
        unit = step * count + number
        grad = jnp.where(layer == 0, grad0[first_units[0] + unit], grad1[first_units[1] + unit])
        if by_rows:
            block = (0, slice(number * rows, (number + 1) * rows), slice(None))
        else:
            block = (0, slice(None), slice(number * width, (number + 1) * width))
        results = adam_step(
            weight[block], first[block], second[block], grad, factor[0], weight_decay, rate
        )
        new[block], first_new[block], second_new[block] = results


def adam_step(weight, first, second, grad, factor, decay, rate):
    grad = grad * factor
    first_new = first_decay * first + (1.0 - first_decay) * grad
    second_new = second_decay * second + (1.0 - second_decay) * grad * grad
    ratio = (
        first_new
        / (1.0 - first_decay**STEP)
        / (jnp.sqrt(second_new / (1.0 - second_decay**STEP)) + adam_epsilon)
    )
    return (weight - rate * (ratio + decay * weight), first_new, second_new)


def kernel_call(body, scalars, arrays, others, outs, package_outs, scratch, flops, aliases=None):
    vmem = pl.BlockSpec(memory_space=pltpu.VMEM)
    anywhere = pl.BlockSpec(memory_space=pl.ANY)
    moved = sum(v.size * v.dtype.itemsize for v in list(arrays) + list(outs) + list(package_outs))
    return pl.pallas_call(
        body,
        in_specs=[pl.BlockSpec(memory_space=pltpu.SMEM)] * len(scalars)
        + [vmem] * len(arrays)
        + [anywhere] * len(others),
        out_specs=[vmem] * len(outs) + [anywhere] * len(package_outs),
        out_shape=list(outs) + list(package_outs),
        scratch_shapes=scratch,
        input_output_aliases=aliases or {},
        compiler_params=pltpu.CompilerParams(vmem_limit_bytes=VMEM_LIMIT),
        cost_estimate=pl.CostEstimate(flops=flops, bytes_accessed=moved, transcendentals=0),
    )(*scalars, *arrays, *others)


def shaped(shape, dtype):
    return jax.ShapeDtypeStruct(shape, dtype)


def call_pack(w_qkv, w_proj, w_fc1, w_fc2):
    layers, rows, width = w_proj.shape
    out = shaped((layers * LAYER_UNITS, rows, width), bf16)
    return kernel_call(pack_weights, (), (w_qkv, w_proj, w_fc1, w_fc2), (), (out,), (), [], 0)[0]


def call_attention(base, x, mod, packed):
    latents, length, width = x.shape
    tokens = latents * length
    owners, _, rows, _ = packed.shape
    like = lambda columns, dtype: shaped((latents, length, columns), dtype)
    return kernel_call(
        functools.partial(attention_forward, base),
        (),
        (x, mod),
        (packed,),
        (like(width, bf16), like(3 * width, bf16), like(width, bf16), like(width, bf16), like(width, f32)),
        (),
        [pltpu.VMEM((owners, 4, rows, width), bf16), pltpu.SemaphoreType.DMA((4,))],
        2 * tokens * width * 4 * width + 8 * tokens * length * width,
    )


def call_feed_forward(base, x1, mod, packed):
    latents, length, width = x1.shape
    owners, _, rows, _ = packed.shape
    like = lambda count, dtype: shaped((latents, length, count), dtype)
    return kernel_call(
        functools.partial(feed_forward, base),
        (),
        (x1, mod),
        (packed,),
        (like(width, bf16), like(FC_UNITS * width, bf16), like(width, bf16), like(width, f32)),
        (),
        [
            pltpu.VMEM((owners, 2 * FC_UNITS, rows, width), bf16),
            pltpu.VMEM((latents * length, width), f32),
            pltpu.SemaphoreType.DMA((2 * FC_UNITS,)),
        ],
        2 * latents * length * width * 2 * FC_UNITS * width,
    )


def call_back(
    body, base, here, arrays, packed, after, outs, package_outs, held_units, units, scratch, flops, aliases=None
):
    owners, _, rows, width = packed.shape
    load_sem = pltpu.SemaphoreType.DMA((2 * FC_UNITS,)) if body is lower_back else pltpu.SemaphoreType.DMA
    return kernel_call(
        functools.partial(body, base, len(package_outs)),
        (here,),
        arrays,
        (packed, *after),
        outs,
        package_outs,
        [pltpu.VMEM((owners, held_units, rows, width), bf16), pltpu.VMEM((owners, units, rows, width), bf16)]
        + scratch
        + [load_sem, pltpu.SemaphoreType.DMA((2,))],
        flops,
        aliases,
    )


def call_lower_back(base, here, d2, mod, u, m, packed, after, package_outs):
    latents, length, width = d2.shape
    tokens = latents * length
    return call_back(
        lower_back, base, here, (d2, mod, u, m), packed, after,
        (shaped(u.shape, bf16), shaped((latents, 1, width), f32)), package_outs,
        FC_UNITS, FC_UNITS,
        [pltpu.VMEM((tokens, width), bf16), pltpu.VMEM((tokens, width), bf16)],
        4 * tokens * width * FC_UNITS * width,
    )


def call_upper_back(base, here, d2, x1, mod, xm2, du, o, a, packed, after, package_outs):
    latents, length, width = x1.shape
    return call_back(
        upper_back, base, here, (d2, x1, mod, xm2, du, o, a), packed, after,
        (shaped(x1.shape, f32), shaped((latents, 3, width), f32), shaped(x1.shape, bf16)), package_outs,
        FC_UNITS, FC_UNITS + 1,
        [pltpu.VMEM((latents * length, width), f32)],
        4 * latents * length * width * FC_UNITS * width,
    )


def call_attention_back(base, here, d1, x, mod, xm, qkv, da, packed, after, package_outs, beside=None):
    latents, length, width = x.shape
    tokens = latents * length
    arrays = (d1, x, mod, xm, qkv, da)
    offset, aliases = 0, None
    if beside is not None:
        offset, aliases = FC_UNITS + 1, {2 + len(arrays) + len(after): 2}
        after = (*after, beside)
        package_outs = (shaped(beside.shape, bf16),)
    return call_back(
        functools.partial(attention_back, offset), base, here, arrays, packed, after,
        (shaped(x.shape, f32), shaped((latents, 2, width), f32)), package_outs,
        4, 3,
        [
            pltpu.VMEM((tokens, width), bf16),
            pltpu.VMEM((tokens, 3 * width), bf16),
            pltpu.VMEM((tokens, width), f32),
        ],
        14 * tokens * width * width + 40 * tokens * length * width,
        aliases,
    )


def call_update(first_units, by_rows, rate, factor, weight, first, second, grad0, grad1):
    rows, width = grad0.shape[1:]
    layers, height, breadth = weight.shape
    steps = 2 if height * breadth > 2 * rows * width and height * breadth % (2 * rows * width) == 0 else 1
    if by_rows:
        block = pl.BlockSpec((1, height // steps, breadth), lambda layer, step: (layer, step, 0))
    else:
        block = pl.BlockSpec((1, height, breadth // steps), lambda layer, step: (layer, 0, step))
    whole = pl.BlockSpec(memory_space=pltpu.VMEM)
    return pl.pallas_call(
        functools.partial(update, first_units, by_rows, rate),
        grid=(layers, steps),
        in_specs=[pl.BlockSpec(memory_space=pltpu.SMEM), block, block, block, whole, whole],
        out_specs=[block] * 3,
        out_shape=[shaped(weight.shape, f32)] * 3,
        compiler_params=pltpu.CompilerParams(vmem_limit_bytes=VMEM_LIMIT),
    )(factor, weight, first, second, grad0, grad1)


def square_sum(*refs):
    total = jnp.float32(0.0)
    for ref in refs[:-1]:
        if len(ref.shape) == 3:
            inner = jnp.zeros(ref.shape[1:], f32)
            for number in range(ref.shape[0]):
                inner = inner + ref[number] * ref[number]
            total = total + jnp.sum(inner)
        else:
            total = total + jnp.sum(ref[...] * ref[...])
    refs[-1][...] = jnp.full(refs[-1].shape, total)


def call_square_sum(arrays):
    return kernel_call(square_sum, (), arrays, (), (shaped((8, 128), f32),), (), [], 0)[0][0, 0]


def nothing(*refs):
    pass


def fence(arrays):
    anywhere = pl.BlockSpec(memory_space=pl.ANY)
    return pl.pallas_call(
        nothing,
        in_specs=[anywhere] * len(arrays),
        out_specs=[anywhere] * len(arrays),
        out_shape=[shaped(array.shape, array.dtype) for array in arrays],
        input_output_aliases={number: number for number in range(len(arrays))},
    )(*arrays)


def swap(value, axis, bit):
    return lax.ppermute(value, axis, [(i, i ^ bit) for i in range(lax.axis_size(axis))])


def double(value, axis, bit):
    return jnp.concatenate([value, swap(value, axis, bit)])


def gather_bits(value, axis):
    held = value[None]
    bit = 1
    while bit < lax.axis_size(axis):
        held = double(held, axis, bit)
        bit *= 2
    return held


def scatter_bits(value, axis):
    bit = 1
    while bit < lax.axis_size(axis):
        halves = value.reshape((value.shape[0] // 2, 2) + value.shape[1:])
        value = halves[:, 0] + swap(halves[:, 1], axis, bit)
        bit *= 2
    return value[0]


def ordered(value, axis):
    me, bit, shape = lax.axis_index(axis), 1, value.shape
    while bit < shape[0]:
        halves = value.reshape((shape[0] // (2 * bit), 2, bit) + shape[1:])
        value = jnp.where((me // bit) % 2 == 1, halves[:, ::-1], halves).reshape(shape)
        bit *= 2
    return value


def tree_sum(values):
    while values.shape[0] > 1:
        values = values.reshape(-1, 2)
        values = values[:, 0] + values[:, 1]
    return values[0]


def sum_bits(value, axis):
    bit = 1
    while bit < lax.axis_size(axis):
        value = value + swap(value, axis, bit)
        bit *= 2
    return value


class Package:
    def __init__(self, arrays, steps, by_place):
        self.arrays, self.by_place = arrays, by_place
        self.split = "x" in steps[0]
        self.steps = ["core"] + steps + ["end"] if by_place else []
        self.held = None

    def offload(self):
        self.held = lax.psum_scatter(self.arrays[0], "shard", scatter_dimension=0)
        self.steps, self.split, self.by_place = ["end"], False, True

    def step(self):
        if not self.steps:
            return
        kind = self.steps.pop(0)
        held = self.held
        if kind == "core":
            keep, send = self.arrays
            self.held = keep + swap(send, "shard", 1)
            if not self.split:
                self.held = self.held[0]
        elif kind == "x":
            self.held = held[0] + swap(held[1], "rep", 1)
        elif kind == "xy":
            owners = lax.axis_size("shard")
            across = [(i, (i ^ owners) ^ 2) for i in range(2 * owners)]
            self.held = (
                (held[0, :4] + swap(held[1, :4], "rep", 1))
                + swap(held[0, 4:], "shard", 2)
                + lax.ppermute(held[1, 4:], ("rep", "shard"), across)
            )
        elif kind == "z":
            self.held = (
                (held[:1] + swap(held[2:3], "shard", 4))
                + swap(held[1:2], "shard", 8)
                + swap(held[3:4], "shard", 12)
            )
        elif kind == "end":
            held = held.reshape(held.shape[-3:])
            other = swap(held, "rep", 1)
            if self.split:
                first = lax.axis_index("rep") == 0
                self.held = jnp.concatenate(
                    [jnp.where(first, held, other), jnp.where(first, other, held)], 2
                ).astype(f32)
            else:
                self.held = held.astype(f32) + other.astype(f32)
        else:
            half = held.shape[0] // 2
            bit = {"y": 2, "near": 4, "far": 8}[kind]
            self.held = held[:half] + swap(held[half:], "shard", bit)

    def finish(self):
        while self.steps:
            self.step()
        if not self.by_place:
            share = scatter_bits(ordered(self.arrays[0], "shard"), "shard")
            self.held = sum_bits(share.astype(f32), "rep")
        return self.held


def package_shapes(packed, units, split, by_place):
    owners, _, rows, width = packed.shape
    if not by_place:
        return (shaped((owners, units, rows, width), bf16),)
    parts = 2 if split else 1
    return (shaped((parts, 8, units, rows, width // parts), bf16),) * 2


def local(tokens, condition, cotangent, *states):
    masters, firsts, seconds = (states[0:6], states[6:12], states[12:18])
    w_ada, b_ada, w_qkv, w_proj, w_fc1, w_fc2 = masters
    owners = lax.axis_size("shard")
    replicas = lax.axis_size("rep")
    me = lax.axis_index("shard")
    here = jnp.stack([me, lax.axis_index("rep")]).astype(jnp.int32)
    batch, length, width = tokens.shape
    part = w_qkv.shape[1]
    by_place = owners == 16 and replicas == 2

    packed = lax.all_gather(call_pack(w_qkv, w_proj, w_fc1, w_fc2), "shard", axis=0)

    cond_act = jax.nn.silu(condition).astype(bf16)
    cond_rep = gather_bits(cond_act, "shard")
    cond_all = ordered(gather_bits(cond_rep, "rep"), "rep")
    cond_mine = lax.dynamic_slice_in_dim(cond_rep, me * part, part, 2).reshape(-1, part)
    cond_mine_all = lax.dynamic_slice_in_dim(cond_all, me * part, part, 3).reshape(-1, part)
    ada_low = w_ada.astype(bf16)
    bias_low = b_ada.astype(bf16).astype(f32)
    shares = []
    for index in range(LAYERS):
        share = jnp.dot(cond_mine, ada_low[index], preferred_element_type=f32)
        bias = lax.dynamic_update_slice(jnp.zeros((6, width), f32), bias_low[index], (0, me * part))
        shares.append(share.reshape(owners, batch, 6, width) + bias)
    modul = scatter_bits(jnp.stack(shares, 2), "shard")

    stream = tokens
    kept = []
    for index in range(LAYERS):
        mod = modul[:, index]
        base = index * LAYER_UNITS
        xm, qkv, o, a, x1 = call_attention(base, stream, mod, packed)
        xm2, u, m, x2 = call_feed_forward(base, x1, mod, packed)
        kept.append((stream, mod, xm, qkv, o, a, x1, xm2, u, m))
        stream = x2
    result = stream.astype(bf16)

    grad = cotangent
    lower, upper, attention = ([None] * LAYERS, [None] * LAYERS, [None] * LAYERS)
    d_modul = [None] * LAYERS
    whole = lambda units: package_shapes(packed, units, False, False)
    after = []
    rounds = []
    for index in reversed(range(LAYERS)):
        x, mod, xm, qkv, o, a, x1, xm2, u, m = kept[index]
        base = index * LAYER_UNITS
        last = index == 0 and by_place
        steps = ["y", "near", "far"]
        du, d_gate, *arrays = call_lower_back(
            base, here, grad, mod, u, m, packed, [],
            package_shapes(packed, FC_UNITS, False, True) if last else whole(FC_UNITS),
        )
        lower[index] = Package(arrays, steps, last)
        if last:
            lower[index].step()
        elif by_place:
            lower[index].offload()
        steps = ["xy", "z"]
        d1, d_middle, da, *arrays = call_upper_back(
            base, here, grad, x1, mod, xm2, du, o, a, packed, [],
            package_shapes(packed, FC_UNITS + 1, True, True) if last else whole(FC_UNITS + 4),
        )
        if last:
            lower[index].held, *arrays = fence([lower[index].held, *arrays])
            after = [lower[index].held]
            lower[index].step()
        upper[index] = Package(arrays, steps, last)
        if last:
            upper[index].step()
        grad, d_first, *arrays = call_attention_back(
            base, here, d1, x, mod, xm, qkv, da, packed, after,
            package_shapes(packed, 3, True, True) if last else (), None if last else arrays[0],
        )
        d_modul[index] = jnp.concatenate([d_first, d_middle, d_gate], 1)
        if last:
            attention[index] = Package(arrays, steps, last)
            rounds = [lower[index], upper[index], attention[index]]
        else:
            upper[index] = attention[index] = Package(arrays, steps, last)
            if by_place:
                upper[index].offload()

    flat = jnp.stack(d_modul, 1).astype(bf16).reshape(1, batch, LAYERS, 6 * width)
    hops = [("shard", 1 << bit) for bit in range(owners.bit_length() - 1)]
    hops += [("rep", 1 << bit) for bit in range(replicas.bit_length() - 1)]
    if rounds:
        held = fence([flat, lower[0].held, upper[0].held, *attention[0].arrays])
        flat, lower[0].held, upper[0].held, *attention[0].arrays = held
    while hops or any(package.steps for package in rounds):
        busy = [package for package in rounds if package.steps]
        for package in busy:
            package.step()
        for axis, bit in hops[:2]:
            flat = double(flat, axis, bit)
        hops = hops[2:]
        results = fence([flat] + [package.held for package in busy])
        flat = results[0]
        for package, held in zip(busy, results[1:]):
            package.held = held
    moving = lower + [upper[0]] + ([attention[0]] if attention[0] is not upper[0] else []) + upper[1:]
    for package in moving:
        package.finish()
    flat_all = ordered(flat.reshape(replicas, owners * batch, LAYERS, 6 * width), "rep")
    flat_all = flat_all.reshape(-1, LAYERS, 6 * width)
    grad_ada = jnp.einsum(
        "bd,blj->ldj", cond_mine_all.reshape(-1, part), flat_all, preferred_element_type=f32
    )
    totals = jnp.sum(flat_all.astype(f32), 0).reshape(LAYERS, 6, width)
    grad_bias = lax.dynamic_slice_in_dim(totals, me * part, part, 2)
    d_cond = jnp.einsum(
        "blj,ldj->bd", flat[:owners].reshape(-1, LAYERS, 6 * width), ada_low, preferred_element_type=f32
    )
    squares = call_square_sum([grad_ada, grad_bias] + [package.held for package in moving])
    told = jnp.concatenate([d_cond, jnp.broadcast_to(squares, (1, part))])
    told = gather_bits(told, "shard")
    grad_norm = jnp.sqrt(tree_sum(told[:, -1, 0]))
    d_cond_mine = jnp.stack([told[i, i * batch : (i + 1) * batch] for i in range(owners)])
    grad_cond_act = ordered(d_cond_mine, "shard").transpose(1, 0, 2).reshape(batch, width)
    unused, silu_back = jax.vjp(jax.nn.silu, condition)
    grad_condition = silu_back(grad_cond_act)[0]
    factor = jnp.minimum(1.0, clip_scale * math.sqrt(PARAMS) / grad_norm)
    updated = []
    for kind, array in ((0, grad_ada), (1, grad_bias)):
        updated.append(
            adam_step(
                masters[kind],
                firsts[kind],
                seconds[kind],
                array,
                factor,
                0.0 if kind == 1 else weight_decay,
                learn_rates[kind],
            )
        )
    behind = [FC_UNITS + 1 if attention[index] is upper[index] else 0 for index in range(LAYERS)]
    for kind, packages, first_units in (
        (2, attention, behind),
        (3, upper, [FC_UNITS] * 2),
        (4, upper, [0] * 2),
        (5, lower, [0] * 2),
    ):
        updated.append(
            call_update(
                first_units,
                kind == 5,
                learn_rates[kind],
                factor.reshape(1),
                masters[kind],
                firsts[kind],
                seconds[kind],
                packages[0].held,
                packages[1].held,
            )
        )
    news, next_firsts, next_seconds = zip(*updated)
    return (result, grad, grad_condition, *news, *next_firsts, *next_seconds, grad_norm)


def solution(mesh):
    latents = P(("rep", "shard"), None, None)
    weights = (P(None, "shard", None), P(None, None, "shard")) + (P(None, "shard", None),) * 4
    in_specs = (latents, P(("rep", "shard"), None), latents) + weights * 3
    out_specs = (latents, latents, P(("rep", "shard"), None)) + weights * 3 + (P(),)
    return jax.shard_map(local, mesh=mesh, in_specs=in_specs, out_specs=out_specs, check_vma=False)
```

```python
import functools
import math

import jax
import jax.numpy as jnp
from jax import lax
from jax.experimental import pallas as pl
from jax.experimental.pallas import tpu as pltpu
from jax.sharding import PartitionSpec as P

HEAD_DIM = 64
LAYERS = 2
STEP = 10
PARAMS = 21242880
FC_UNITS = 4
LAYER_UNITS = 12
PROJ, FC1, FC2 = 3, 4, 8
VMEM_LIMIT = 56 * 1024 * 1024

norm_epsilon = 1e-06
first_decay = 0.9
second_decay = 0.95
learn_rates = (0.03, 1.0, 0.03, 0.1, 0.03, 0.03)
weight_decay = 0.1
adam_epsilon = 1e-08
clip_scale = 0.5

f32 = jnp.float32
bf16 = jnp.bfloat16


def dot_nn(left, right):
    return lax.dot_general(left, right, (((1,), (0,)), ((), ())), preferred_element_type=f32)


def dot_nt(left, right):
    return lax.dot_general(left, right, (((1,), (1,)), ((), ())), preferred_element_type=f32)


def dot_tn(left, right):
    return lax.dot_general(left, right, (((0,), (0,)), ((), ())), preferred_element_type=f32)


def matrix(block):
    rows, width = block.shape[-2:]
    if rows % 16 == 0:
        return block.reshape(-1, width)
    return block.astype(f32).reshape(-1, width).astype(block.dtype)


def load_weights(packed, first, held, sem):
    copy = pltpu.make_async_copy(packed.at[:, pl.ds(first, held.shape[1])], held, sem)
    copy.start()
    return copy.wait


def store_grads(here, grads, outs, sems, unit, units, first=0, number=None, offset=0):
    number = grads.shape[0] if number is None else number
    chosen = pl.ds(unit, units)
    if len(outs) == 1:
        owners = pl.ds(first, number)
        pltpu.make_async_copy(
            grads.at[owners, chosen], outs[0].at[owners, pl.ds(offset + unit, units)], sems.at[0]
        ).start()
        return
    parts, places, _, _, width = outs[0].shape
    for step in range(number):
        owner = first + step
        other = owner ^ here[0]
        place = 4 * ((other >> 1) & 1) + 2 * ((other >> 2) & 1) + ((other >> 3) & 1)
        for core in range(2):

            @pl.when((other & 1) == core)
            def _():
                for turn in range(parts):
                    column = pl.multiple_of((turn ^ here[1]) * width, 128) if parts > 1 else 0
                    pltpu.make_async_copy(
                        grads.at[owner, chosen, :, pl.ds(column, width)],
                        outs[core].at[turn, place, chosen],
                        sems.at[core],
                    ).start()


def wait_grads(outs, sems, units, offset=0):
    for number, out in enumerate(outs):
        if len(outs) == 1:
            out = out.at[:, pl.ds(offset, units)]
        pltpu.make_async_copy(out, out, sems.at[number]).wait()


def weight_grad(left, right, grads, unit):
    owners, _, rows, width = grads.shape
    grads[:, unit] = dot_tn(left, right).reshape(owners, rows, width).astype(bf16)


def flat(value):
    return value.reshape(-1, value.shape[-1])


def pack_weights(qkv, proj, fc1, fc2, packed):
    rows, width = packed.shape[1:]
    for layer in range(qkv.shape[0]):
        base = layer * LAYER_UNITS
        for unit in range(PROJ):
            packed[base + unit] = qkv[layer, :, unit * width : (unit + 1) * width].astype(bf16)
        packed[base + PROJ] = proj[layer].astype(bf16)
        for unit in range(FC_UNITS):
            packed[base + FC1 + unit] = fc1[layer, :, unit * width : (unit + 1) * width].astype(bf16)
            packed[base + FC2 + unit] = fc2[layer, unit * rows : (unit + 1) * rows].astype(bf16)


def normalise(value):
    centred = value - jnp.mean(value, -1, keepdims=True)
    spread = jnp.mean(centred * centred, -1, keepdims=True)
    rate = lax.rsqrt(spread + norm_epsilon)
    return centred * rate, rate


def normalise_back(grad, value, scale):
    unit, rate = normalise(value)
    d_shift = jnp.sum(grad, 0, keepdims=True)
    d_scale = jnp.sum(grad * unit, 0, keepdims=True)
    inner = grad * (1.0 + scale)
    d_value = rate * (
        inner
        - jnp.mean(inner, -1, keepdims=True)
        - unit * jnp.mean(inner * unit, -1, keepdims=True)
    )
    return d_value, d_shift, d_scale


def head_masks(rows):
    lane = lax.broadcasted_iota(jnp.int32, (rows, 2 * HEAD_DIM), 1)
    return lane < HEAD_DIM, lane >= HEAD_DIM


def pick(mask, value):
    return jnp.where(mask, value, jnp.zeros_like(value))


def attention_forward(base, x, mod, packed, xm, qkv, o, a, x1, held, sems):
    waits = [load_weights(packed, base + unit, held.at[:, pl.ds(unit, 1)], sems.at[unit]) for unit in range(4)]
    latents, length, width = x.shape

    @pl.loop(0, latents)
    def _(lat):
        unit, _ = normalise(x[lat].astype(f32))
        xm[lat] = (unit * (1.0 + mod[lat, 1:2, :]) + mod[lat, 0:1, :]).astype(bf16)

    for block in range(3):
        waits[block]()
        product = dot_nn(flat(xm[...]), matrix(held[:, block])).astype(bf16)
        qkv[:, :, block * width : (block + 1) * width] = product.reshape(latents, length, width)

    @pl.loop(0, latents)
    def _(lat):
        @pl.loop(0, width // (2 * HEAD_DIM))
        def _(pair):
            lanes = 2 * HEAD_DIM
            start = pl.multiple_of(pair * lanes, lanes)
            query = qkv[lat, :, pl.ds(start, lanes)] * bf16(HEAD_DIM**-0.5)
            keys = qkv[lat, :, pl.ds(width + start, lanes)]
            values = qkv[lat, :, pl.ds(2 * width + start, lanes)]
            total = jnp.zeros((length, lanes), f32)
            for mask in head_masks(length):
                scores = dot_nt(pick(mask, query), keys)
                expo = jnp.exp(scores - jnp.max(scores, -1, keepdims=True))
                probs = (expo * (1.0 / jnp.sum(expo, -1, keepdims=True))).astype(bf16)
                total = total + dot_nn(probs, pick(mask, values))
            o[lat, :, pl.ds(start, lanes)] = total.astype(bf16)

    waits[PROJ]()
    branch = dot_nn(flat(o[...]), matrix(held[:, PROJ])).reshape(latents, length, width)
    for lat in range(latents):
        a[lat] = branch[lat].astype(bf16)
        x1[lat] = x[lat].astype(f32) + mod[lat, 2:3, :] * branch[lat]


def gelu_parts(value):
    c = math.sqrt(2.0 / math.pi)
    square = value * value
    tanh = jnp.tanh(c * value * (1.0 + 0.044715 * square))
    half = 0.5 * (1.0 + tanh)
    slope = half + 0.5 * value * (1.0 - tanh * tanh) * c * (1.0 + 3.0 * 0.044715 * square)
    return value * half, slope


def load_feed_forward(packed, base, held, sems):
    share = held.shape[0] // FC_UNITS
    both = held.shape[1] > FC_UNITS
    for block in range(FC_UNITS):
        if both:
            load_weights(packed, base + FC1 + block, held.at[:, pl.ds(block, 1)], sems.at[block])
        owners = pl.ds(block * share, share)
        units = pl.ds(held.shape[1] - FC_UNITS, FC_UNITS)
        pltpu.make_async_copy(
            packed.at[owners, pl.ds(base + FC2, FC_UNITS)], held.at[owners, units], sems.at[FC_UNITS + block]
        ).start()

    def wait_upper(block):
        column = held.at[:, pl.ds(block, 1)]
        pltpu.make_async_copy(column, column, sems.at[block]).wait()

    def wait_lower(block):
        rows = held.at[pl.ds(block * share, share), pl.ds(held.shape[1] - FC_UNITS, FC_UNITS)]
        pltpu.make_async_copy(rows, rows, sems.at[FC_UNITS + block]).wait()

    return wait_upper, wait_lower


def feed_forward(base, x1, mod, packed, xm2, u, m, x2, held, total, sems):
    wait_upper, wait_lower = load_feed_forward(packed, base, held, sems)
    latents, length, width = x1.shape
    share = held.shape[0] // FC_UNITS

    @pl.loop(0, latents)
    def _(lat):
        unit, _ = normalise(x1[lat])
        xm2[lat] = (unit * (1.0 + mod[lat, 4:5, :]) + mod[lat, 3:4, :]).astype(bf16)

    total[...] = jnp.zeros_like(total)

    @pl.loop(0, FC_UNITS)
    def _(block):
        columns = pl.ds(pl.multiple_of(block * width, 128), width)
        wait_upper(block)
        upper = dot_nn(flat(xm2[...]), matrix(held[:, block]))
        u[:, :, columns] = upper.astype(bf16).reshape(latents, length, width)
        active = gelu_parts(upper)[0].astype(bf16)
        wait_lower(block)
        total[...] += dot_nn(active, matrix(held[pl.ds(block * share, share), FC_UNITS:]))

    for lat in range(latents):
        result = total[lat * length : (lat + 1) * length, :]
        m[lat] = result.astype(bf16)
        x2[lat] = x1[lat] + mod[lat, 5:6, :] * result


def lower_back(base, given, here, d2, mod, u, m, packed, *refs):
    refs = refs[-(8 + given) :]
    du, dgate = refs[:2]
    outs, (held, grads, dm, active, load_sems, sems) = refs[2 : 2 + given], refs[2 + given :]
    _, wait_lower = load_feed_forward(packed, base, held, load_sems)
    latents, length, width = d2.shape
    owners, _, part, _ = held.shape
    share = owners // FC_UNITS

    @pl.loop(0, latents)
    def _(lat):
        rows = pl.ds(pl.multiple_of(lat * length, length), length)
        grad = d2[lat].astype(f32)
        dgate[lat] = jnp.sum(grad * m[lat].astype(f32), 0, keepdims=True)
        dm[rows, :] = (grad * mod[lat, 5:6, :]).astype(bf16)

    @pl.loop(0, FC_UNITS)
    def _(block):
        columns = pl.ds(pl.multiple_of(block * width, 128), width)
        shards = pl.ds(block * share, share)
        wait_lower(block)
        d_active = dot_nt(dm[...], matrix(held[shards]))
        value, slope = gelu_parts(flat(u[:, :, columns]).astype(f32))
        active[...] = value.astype(bf16)
        du[:, :, columns] = (d_active * slope).astype(bf16).reshape(latents, length, width)
        grads[shards] = dot_tn(active[...], dm[...]).reshape(share, FC_UNITS, part, width).astype(bf16)
        store_grads(here, grads, outs, sems, 0, FC_UNITS, block * share, share)

    wait_grads(outs, sems, FC_UNITS)


def upper_back(base, given, here, d2, x1, mod, xm2, du, o, a, packed, *refs):
    refs = refs[-(8 + given) :]
    d1, dmod, da = refs[:3]
    outs, (held, grads, total, sem, sems) = refs[3 : 3 + given], refs[3 + given : 8 + given]
    wait = load_weights(packed, base + FC1, held, sem)
    latents, length, width = x1.shape
    tokens = latents * length

    @pl.loop(0, FC_UNITS)
    def _(block):
        columns = pl.ds(pl.multiple_of(block * width, 128), width)
        weight_grad(flat(xm2[...]), flat(du[:, :, columns]), grads, block)

    store_grads(here, grads, outs, sems, 0, FC_UNITS)
    wait()
    total[...] = jnp.zeros_like(total)

    @pl.loop(0, FC_UNITS)
    def _(block):
        columns = pl.ds(pl.multiple_of(block * width, 128), width)
        total[...] += dot_nt(flat(du[:, :, columns]), matrix(held[:, block]))

    @pl.loop(0, latents)
    def _(lat):
        rows = pl.ds(pl.multiple_of(lat * length, length), length)
        back, d_shift, d_scale = normalise_back(total[rows, :], x1[lat], mod[lat, 4:5, :])
        grad = d2[lat].astype(f32) + back
        dmod[lat, 1:2, :] = d_shift
        dmod[lat, 2:3, :] = d_scale
        dmod[lat, 0:1, :] = jnp.sum(grad * a[lat].astype(f32), 0, keepdims=True)
        d1[lat] = grad
        da[lat] = (grad * mod[lat, 2:3, :]).astype(bf16)

    weight_grad(flat(o[...]), flat(da[...]), grads, FC_UNITS)
    store_grads(here, grads, outs, sems, FC_UNITS, 1)
    wait_grads(outs, sems, FC_UNITS + 1)


def attention_back(offset, base, given, here, d1, x, mod, xm, qkv, da, packed, *refs):
    refs = refs[-(9 + given) :]
    d0, dmod = refs[:2]
    outs, (held, grads, do, dqkv, total, sem, sems) = refs[2 : 2 + given], refs[2 + given :]
    wait = load_weights(packed, base, held, sem)
    latents, length, width = x.shape
    tokens = latents * length
    lanes = 2 * HEAD_DIM
    wait()
    do[...] = dot_nt(flat(da[...]), matrix(held[:, PROJ])).astype(bf16)

    @pl.loop(0, latents)
    def _(lat):
        rows = pl.ds(pl.multiple_of(lat * length, length), length)

        @pl.loop(0, width // lanes)
        def _(pair):
            start = pl.multiple_of(pair * lanes, lanes)
            query = qkv[lat, :, pl.ds(start, lanes)] * bf16(HEAD_DIM**-0.5)
            keys = qkv[lat, :, pl.ds(width + start, lanes)]
            values = qkv[lat, :, pl.ds(2 * width + start, lanes)]
            d_out = do[rows, pl.ds(start, lanes)]
            d_query = jnp.zeros((length, lanes), f32)
            d_keys = jnp.zeros((length, lanes), f32)
            d_values = jnp.zeros((length, lanes), f32)
            for mask in head_masks(length):
                own_query, own_out = pick(mask, query), pick(mask, d_out)
                scores = dot_nt(keys, own_query)
                expo = jnp.exp(scores - jnp.max(scores, 0, keepdims=True))
                probs = expo * (1.0 / jnp.sum(expo, 0, keepdims=True))
                d_values = d_values + dot_nn(probs.astype(bf16), own_out)
                d_probs = dot_nt(values, own_out)
                inner = jnp.sum(d_probs * probs, 0, keepdims=True)
                d_scores = (probs * (d_probs - inner)).astype(bf16)
                d_keys = d_keys + dot_nn(d_scores, own_query)
                d_query = d_query + dot_tn(d_scores, pick(mask, keys))
            dqkv[rows, pl.ds(start, lanes)] = (d_query * HEAD_DIM**-0.5).astype(bf16)
            dqkv[rows, pl.ds(width + start, lanes)] = d_keys.astype(bf16)
            dqkv[rows, pl.ds(2 * width + start, lanes)] = d_values.astype(bf16)

    @pl.loop(0, 3)
    def _(block):
        columns = pl.ds(pl.multiple_of(block * width, 128), width)
        weight_grad(flat(xm[...]), dqkv[:, columns], grads, block)

    store_grads(here, grads, outs, sems, 0, 3, offset=offset)

    total[...] = jnp.zeros_like(total)

    @pl.loop(0, 3)
    def _(block):
        columns = pl.ds(pl.multiple_of(block * width, 128), width)
        total[...] += dot_nt(dqkv[:, columns], matrix(held[:, block]))

    @pl.loop(0, latents)
    def _(lat):
        rows = pl.ds(pl.multiple_of(lat * length, length), length)
        back, d_shift, d_scale = normalise_back(total[rows, :], x[lat].astype(f32), mod[lat, 1:2, :])
        dmod[lat, 0:1, :] = d_shift
        dmod[lat, 1:2, :] = d_scale
        d0[lat] = d1[lat] + back

    wait_grads(outs, sems, 3, offset)


def update(first_units, by_rows, rate, factor, weight, first, second, grad0, grad1, new, first_new, second_new):
    layer, step = pl.program_id(0), pl.program_id(1)
    rows, width = grad0.shape[1:]
    count = weight.shape[1] * weight.shape[2] // (rows * width)
    for number in range(count):
        unit = step * count + number
        grad = jnp.where(layer == 0, grad0[first_units[0] + unit], grad1[first_units[1] + unit])
        if by_rows:
            block = (0, slice(number * rows, (number + 1) * rows), slice(None))
        else:
            block = (0, slice(None), slice(number * width, (number + 1) * width))
        results = adam_step(
            weight[block], first[block], second[block], grad, factor[0], weight_decay, rate
        )
        new[block], first_new[block], second_new[block] = results


def adam_step(weight, first, second, grad, factor, decay, rate):
    grad = grad * factor
    first_new = first_decay * first + (1.0 - first_decay) * grad
    second_new = second_decay * second + (1.0 - second_decay) * grad * grad
    ratio = (
        first_new
        / (1.0 - first_decay**STEP)
        / (jnp.sqrt(second_new / (1.0 - second_decay**STEP)) + adam_epsilon)
    )
    return (weight - rate * (ratio + decay * weight), first_new, second_new)


def kernel_call(body, scalars, arrays, others, outs, package_outs, scratch, flops, aliases=None):
    vmem = pl.BlockSpec(memory_space=pltpu.VMEM)
    anywhere = pl.BlockSpec(memory_space=pl.ANY)
    moved = sum(v.size * v.dtype.itemsize for v in list(arrays) + list(outs) + list(package_outs))
    return pl.pallas_call(
        body,
        in_specs=[pl.BlockSpec(memory_space=pltpu.SMEM)] * len(scalars)
        + [vmem] * len(arrays)
        + [anywhere] * len(others),
        out_specs=[vmem] * len(outs) + [anywhere] * len(package_outs),
        out_shape=list(outs) + list(package_outs),
        scratch_shapes=scratch,
        input_output_aliases=aliases or {},
        compiler_params=pltpu.CompilerParams(vmem_limit_bytes=VMEM_LIMIT),
        cost_estimate=pl.CostEstimate(flops=flops, bytes_accessed=moved, transcendentals=0),
    )(*scalars, *arrays, *others)


def shaped(shape, dtype):
    return jax.ShapeDtypeStruct(shape, dtype)


def call_pack(w_qkv, w_proj, w_fc1, w_fc2):
    layers, rows, width = w_proj.shape
    out = shaped((layers * LAYER_UNITS, rows, width), bf16)
    return kernel_call(pack_weights, (), (w_qkv, w_proj, w_fc1, w_fc2), (), (out,), (), [], 0)[0]


def call_attention(base, x, mod, packed):
    latents, length, width = x.shape
    tokens = latents * length
    owners, _, rows, _ = packed.shape
    like = lambda columns, dtype: shaped((latents, length, columns), dtype)
    return kernel_call(
        functools.partial(attention_forward, base),
        (),
        (x, mod),
        (packed,),
        (like(width, bf16), like(3 * width, bf16), like(width, bf16), like(width, bf16), like(width, f32)),
        (),
        [pltpu.VMEM((owners, 4, rows, width), bf16), pltpu.SemaphoreType.DMA((4,))],
        2 * tokens * width * 4 * width + 8 * tokens * length * width,
    )


def call_feed_forward(base, x1, mod, packed):
    latents, length, width = x1.shape
    owners, _, rows, _ = packed.shape
    like = lambda count, dtype: shaped((latents, length, count), dtype)
    return kernel_call(
        functools.partial(feed_forward, base),
        (),
        (x1, mod),
        (packed,),
        (like(width, bf16), like(FC_UNITS * width, bf16), like(width, bf16), like(width, f32)),
        (),
        [
            pltpu.VMEM((owners, 2 * FC_UNITS, rows, width), bf16),
            pltpu.VMEM((latents * length, width), f32),
            pltpu.SemaphoreType.DMA((2 * FC_UNITS,)),
        ],
        2 * latents * length * width * 2 * FC_UNITS * width,
    )


def call_back(
    body, base, here, arrays, packed, after, outs, package_outs, held_units, units, scratch, flops, aliases=None
):
    owners, _, rows, width = packed.shape
    load_sem = pltpu.SemaphoreType.DMA((2 * FC_UNITS,)) if body is lower_back else pltpu.SemaphoreType.DMA
    return kernel_call(
        functools.partial(body, base, len(package_outs)),
        (here,),
        arrays,
        (packed, *after),
        outs,
        package_outs,
        [pltpu.VMEM((owners, held_units, rows, width), bf16), pltpu.VMEM((owners, units, rows, width), bf16)]
        + scratch
        + [load_sem, pltpu.SemaphoreType.DMA((2,))],
        flops,
        aliases,
    )


def call_lower_back(base, here, d2, mod, u, m, packed, after, package_outs):
    latents, length, width = d2.shape
    tokens = latents * length
    return call_back(
        lower_back, base, here, (d2, mod, u, m), packed, after,
        (shaped(u.shape, bf16), shaped((latents, 1, width), f32)), package_outs,
        FC_UNITS, FC_UNITS,
        [pltpu.VMEM((tokens, width), bf16), pltpu.VMEM((tokens, width), bf16)],
        4 * tokens * width * FC_UNITS * width,
    )


def call_upper_back(base, here, d2, x1, mod, xm2, du, o, a, packed, after, package_outs):
    latents, length, width = x1.shape
    return call_back(
        upper_back, base, here, (d2, x1, mod, xm2, du, o, a), packed, after,
        (shaped(x1.shape, f32), shaped((latents, 3, width), f32), shaped(x1.shape, bf16)), package_outs,
        FC_UNITS, FC_UNITS + 1,
        [pltpu.VMEM((latents * length, width), f32)],
        4 * latents * length * width * FC_UNITS * width,
    )


def call_attention_back(base, here, d1, x, mod, xm, qkv, da, packed, after, package_outs, beside=None):
    latents, length, width = x.shape
    tokens = latents * length
    arrays = (d1, x, mod, xm, qkv, da)
    offset, aliases = 0, None
    if beside is not None:
        offset, aliases = FC_UNITS + 1, {2 + len(arrays) + len(after): 2}
        after = (*after, beside)
        package_outs = (shaped(beside.shape, bf16),)
    return call_back(
        functools.partial(attention_back, offset), base, here, arrays, packed, after,
        (shaped(x.shape, f32), shaped((latents, 2, width), f32)), package_outs,
        4, 3,
        [
            pltpu.VMEM((tokens, width), bf16),
            pltpu.VMEM((tokens, 3 * width), bf16),
            pltpu.VMEM((tokens, width), f32),
        ],
        14 * tokens * width * width + 40 * tokens * length * width,
        aliases,
    )


def call_update(first_units, by_rows, rate, factor, weight, first, second, grad0, grad1):
    rows, width = grad0.shape[1:]
    layers, height, breadth = weight.shape
    steps = 2 if height * breadth > 2 * rows * width and height * breadth % (2 * rows * width) == 0 else 1
    if by_rows:
        block = pl.BlockSpec((1, height // steps, breadth), lambda layer, step: (layer, step, 0))
    else:
        block = pl.BlockSpec((1, height, breadth // steps), lambda layer, step: (layer, 0, step))
    whole = pl.BlockSpec(memory_space=pltpu.VMEM)
    return pl.pallas_call(
        functools.partial(update, first_units, by_rows, rate),
        grid=(layers, steps),
        in_specs=[pl.BlockSpec(memory_space=pltpu.SMEM), block, block, block, whole, whole],
        out_specs=[block] * 3,
        out_shape=[shaped(weight.shape, f32)] * 3,
        compiler_params=pltpu.CompilerParams(vmem_limit_bytes=VMEM_LIMIT),
    )(factor, weight, first, second, grad0, grad1)


def square_sum(*refs):
    total = jnp.float32(0.0)
    for ref in refs[:-1]:
        if len(ref.shape) == 3:
            inner = jnp.zeros(ref.shape[1:], f32)
            for number in range(ref.shape[0]):
                inner = inner + ref[number] * ref[number]
            total = total + jnp.sum(inner)
        else:
            total = total + jnp.sum(ref[...] * ref[...])
    refs[-1][...] = jnp.full(refs[-1].shape, total)


def call_square_sum(arrays):
    return kernel_call(square_sum, (), arrays, (), (shaped((8, 128), f32),), (), [], 0)[0][0, 0]


def nothing(*refs):
    pass


def fence(arrays):
    anywhere = pl.BlockSpec(memory_space=pl.ANY)
    return pl.pallas_call(
        nothing,
        in_specs=[anywhere] * len(arrays),
        out_specs=[anywhere] * len(arrays),
        out_shape=[shaped(array.shape, array.dtype) for array in arrays],
        input_output_aliases={number: number for number in range(len(arrays))},
    )(*arrays)


def swap(value, axis, bit):
    return lax.ppermute(value, axis, [(i, i ^ bit) for i in range(lax.axis_size(axis))])


def double(value, axis, bit):
    return jnp.concatenate([value, swap(value, axis, bit)])


def gather_bits(value, axis):
    held = value[None]
    bit = 1
    while bit < lax.axis_size(axis):
        held = double(held, axis, bit)
        bit *= 2
    return held


def scatter_bits(value, axis):
    bit = 1
    while bit < lax.axis_size(axis):
        halves = value.reshape((value.shape[0] // 2, 2) + value.shape[1:])
        value = halves[:, 0] + swap(halves[:, 1], axis, bit)
        bit *= 2
    return value[0]


def ordered(value, axis):
    me, bit, shape = lax.axis_index(axis), 1, value.shape
    while bit < shape[0]:
        halves = value.reshape((shape[0] // (2 * bit), 2, bit) + shape[1:])
        value = jnp.where((me // bit) % 2 == 1, halves[:, ::-1], halves).reshape(shape)
        bit *= 2
    return value


def tree_sum(values):
    while values.shape[0] > 1:
        values = values.reshape(-1, 2)
        values = values[:, 0] + values[:, 1]
    return values[0]


def sum_bits(value, axis):
    bit = 1
    while bit < lax.axis_size(axis):
        value = value + swap(value, axis, bit)
        bit *= 2
    return value


class Package:
    def __init__(self, arrays, steps, by_place):
        self.arrays, self.by_place = arrays, by_place
        self.split = "x" in steps
        self.steps = ["core"] + steps + ["end"] if by_place else []
        self.held = None

    def offload(self):
        self.held = lax.psum_scatter(self.arrays[0], "shard", scatter_dimension=0)
        self.steps, self.split, self.by_place = ["end"], False, True

    def step(self):
        if not self.steps:
            return
        kind = self.steps.pop(0)
        held = self.held
        if kind == "core":
            keep, send = self.arrays
            self.held = keep + swap(send, "shard", 1)
            if not self.split:
                self.held = self.held[0]
        elif kind == "x":
            self.held = held[0] + swap(held[1], "rep", 1)
        elif kind == "z":
            self.held = (
                (held[:1] + swap(held[2:3], "shard", 4))
                + swap(held[1:2], "shard", 8)
                + swap(held[3:4], "shard", 12)
            )
        elif kind == "end":
            held = held.reshape(held.shape[-3:])
            other = swap(held, "rep", 1)
            if self.split:
                first = lax.axis_index("rep") == 0
                self.held = jnp.concatenate(
                    [jnp.where(first, held, other), jnp.where(first, other, held)], 2
                ).astype(f32)
            else:
                self.held = held.astype(f32) + other.astype(f32)
        else:
            half = held.shape[0] // 2
            self.held = held[:half] + swap(held[half:], "shard", 2)

    def finish(self):
        while self.steps:
            self.step()
        if not self.by_place:
            share = scatter_bits(ordered(self.arrays[0], "shard"), "shard")
            self.held = sum_bits(share.astype(f32), "rep")
        return self.held


def package_shapes(packed, units, split, by_place):
    owners, _, rows, width = packed.shape
    if not by_place:
        return (shaped((owners, units, rows, width), bf16),)
    parts = 2 if split else 1
    return (shaped((parts, 8, units, rows, width // parts), bf16),) * 2


def local(tokens, condition, cotangent, *states):
    masters, firsts, seconds = (states[0:6], states[6:12], states[12:18])
    w_ada, b_ada, w_qkv, w_proj, w_fc1, w_fc2 = masters
    owners = lax.axis_size("shard")
    replicas = lax.axis_size("rep")
    me = lax.axis_index("shard")
    here = jnp.stack([me, lax.axis_index("rep")]).astype(jnp.int32)
    batch, length, width = tokens.shape
    part = w_qkv.shape[1]
    by_place = owners == 16 and replicas == 2

    packed = lax.all_gather(call_pack(w_qkv, w_proj, w_fc1, w_fc2), "shard", axis=0)

    cond_act = jax.nn.silu(condition).astype(bf16)
    cond_rep = gather_bits(cond_act, "shard")
    cond_all = ordered(gather_bits(cond_rep, "rep"), "rep")
    cond_mine = lax.dynamic_slice_in_dim(cond_rep, me * part, part, 2).reshape(-1, part)
    cond_mine_all = lax.dynamic_slice_in_dim(cond_all, me * part, part, 3).reshape(-1, part)
    ada_low = w_ada.astype(bf16)
    bias_low = b_ada.astype(bf16).astype(f32)
    shares = []
    for index in range(LAYERS):
        share = jnp.dot(cond_mine, ada_low[index], preferred_element_type=f32)
        bias = lax.dynamic_update_slice(jnp.zeros((6, width), f32), bias_low[index], (0, me * part))
        shares.append(share.reshape(owners, batch, 6, width) + bias)
    modul = scatter_bits(jnp.stack(shares, 2), "shard")

    stream = tokens
    kept = []
    for index in range(LAYERS):
        mod = modul[:, index]
        base = index * LAYER_UNITS
        xm, qkv, o, a, x1 = call_attention(base, stream, mod, packed)
        xm2, u, m, x2 = call_feed_forward(base, x1, mod, packed)
        kept.append((stream, mod, xm, qkv, o, a, x1, xm2, u, m))
        stream = x2
    result = stream.astype(bf16)

    grad = cotangent
    lower, upper, attention = ([None] * LAYERS, [None] * LAYERS, [None] * LAYERS)
    d_modul = [None] * LAYERS
    whole = lambda units: package_shapes(packed, units, False, False)
    after = []
    rounds = []
    for index in reversed(range(LAYERS)):
        x, mod, xm, qkv, o, a, x1, xm2, u, m = kept[index]
        base = index * LAYER_UNITS
        last = index == 0 and by_place
        steps = ["y", "z"]
        du, d_gate, *arrays = call_lower_back(
            base, here, grad, mod, u, m, packed, [],
            package_shapes(packed, FC_UNITS, False, True) if last else whole(FC_UNITS),
        )
        lower[index] = Package(arrays, steps, last)
        if last:
            lower[index].step()
        elif by_place:
            lower[index].offload()
        steps = ["x", "y", "z"]
        d1, d_middle, da, *arrays = call_upper_back(
            base, here, grad, x1, mod, xm2, du, o, a, packed, [],
            package_shapes(packed, FC_UNITS + 1, True, True) if last else whole(FC_UNITS + 4),
        )
        if last:
            lower[index].held, *arrays = fence([lower[index].held, *arrays])
            lower[index].step()
        upper[index] = Package(arrays, steps, last)
        if last:
            upper[index].step()
            after = upper[index].held, = fence([upper[index].held])
            upper[index].step()
        grad, d_first, *arrays = call_attention_back(
            base, here, d1, x, mod, xm, qkv, da, packed, after,
            package_shapes(packed, 3, True, True) if last else (), None if last else arrays[0],
        )
        d_modul[index] = jnp.concatenate([d_first, d_middle, d_gate], 1)
        if last:
            attention[index] = Package(arrays, steps, last)
            rounds = [lower[index], upper[index], attention[index]]
        else:
            upper[index] = attention[index] = Package(arrays, steps, last)
            if by_place:
                upper[index].offload()

    flat = jnp.stack(d_modul, 1).astype(bf16).reshape(1, batch, LAYERS, 6 * width)
    hops = [("shard", 1 << bit) for bit in range(owners.bit_length() - 1)]
    hops += [("rep", 1 << bit) for bit in range(replicas.bit_length() - 1)]
    if rounds:
        held = fence([flat, lower[0].held, upper[0].held, *attention[0].arrays])
        flat, lower[0].held, upper[0].held, *attention[0].arrays = held
    while hops or any(package.steps for package in rounds):
        busy = [package for package in rounds if package.steps]
        for package in busy:
            package.step()
        taken = 2 if len(hops) > 3 else 1
        for axis, bit in hops[:taken]:
            flat = double(flat, axis, bit)
        hops = hops[taken:]
        results = fence([flat] + [package.held for package in busy])
        flat = results[0]
        for package, held in zip(busy, results[1:]):
            package.held = held
    moving = lower + [upper[0]] + ([attention[0]] if attention[0] is not upper[0] else []) + upper[1:]
    for package in moving:
        package.finish()
    flat_all = ordered(flat.reshape(replicas, owners * batch, LAYERS, 6 * width), "rep")
    flat_all = flat_all.reshape(-1, LAYERS, 6 * width)
    grad_ada = jnp.einsum(
        "bd,blj->ldj", cond_mine_all.reshape(-1, part), flat_all, preferred_element_type=f32
    )
    totals = jnp.sum(flat_all.astype(f32), 0).reshape(LAYERS, 6, width)
    grad_bias = lax.dynamic_slice_in_dim(totals, me * part, part, 2)
    d_cond = jnp.einsum(
        "blj,ldj->bd", flat[:owners].reshape(-1, LAYERS, 6 * width), ada_low, preferred_element_type=f32
    )
    squares = call_square_sum([grad_ada, grad_bias] + [package.held for package in moving])
    told = jnp.concatenate([d_cond, jnp.broadcast_to(squares, (1, part))])
    told = gather_bits(told, "shard")
    grad_norm = jnp.sqrt(tree_sum(told[:, -1, 0]))
    d_cond_mine = jnp.stack([told[i, i * batch : (i + 1) * batch] for i in range(owners)])
    grad_cond_act = ordered(d_cond_mine, "shard").transpose(1, 0, 2).reshape(batch, width)
    unused, silu_back = jax.vjp(jax.nn.silu, condition)
    grad_condition = silu_back(grad_cond_act)[0]
    factor = jnp.minimum(1.0, clip_scale * math.sqrt(PARAMS) / grad_norm)
    updated = []
    for kind, array in ((0, grad_ada), (1, grad_bias)):
        updated.append(
            adam_step(
                masters[kind],
                firsts[kind],
                seconds[kind],
                array,
                factor,
                0.0 if kind == 1 else weight_decay,
                learn_rates[kind],
            )
        )
    behind = [FC_UNITS + 1 if attention[index] is upper[index] else 0 for index in range(LAYERS)]
    for kind, packages, first_units in (
        (2, attention, behind),
        (3, upper, [FC_UNITS] * 2),
        (4, upper, [0] * 2),
        (5, lower, [0] * 2),
    ):
        updated.append(
            call_update(
                first_units,
                kind == 5,
                learn_rates[kind],
                factor.reshape(1),
                masters[kind],
                firsts[kind],
                seconds[kind],
                packages[0].held,
                packages[1].held,
            )
        )
    news, next_firsts, next_seconds = zip(*updated)
    return (result, grad, grad_condition, *news, *next_firsts, *next_seconds, grad_norm)


def solution(mesh):
    latents = P(("rep", "shard"), None, None)
    weights = (P(None, "shard", None), P(None, None, "shard")) + (P(None, "shard", None),) * 4
    in_specs = (latents, P(("rep", "shard"), None), latents) + weights * 3
    out_specs = (latents, latents, P(("rep", "shard"), None)) + weights * 3 + (P(),)
    return jax.shard_map(local, mesh=mesh, in_specs=in_specs, out_specs=out_specs, check_vma=False)
```
